1024 devices in a mesh: dp: 16 (over x, z_hi), space: 64 (over y, z_lo, core).
Axes of the slice: x: 4, y: 4, z: 32 (z_hi: 4, z_lo: 8; z = z_hi * 8 + z_lo), core: 2. Of those that a mesh axis runs over, the one named last changes fastest.
Arguments:
- volume: bfloat16 [16, 128, 8, 64, 128], P('dp', 'space'), may hold values from -6 to 6
- weight: bfloat16 [3, 3, 3, 64, 128], replicated, may hold values from -0.15625 to 0.15625
- cotangent: bfloat16 [16, 64, 4, 64, 128], P('dp', 'space'), may hold values from -6 to 6
Outputs:
- output: bfloat16 [16, 64, 4, 64, 128], P('dp', 'space')
- grad_volume: bfloat16 [16, 128, 8, 64, 128], P('dp', 'space')
- grad_weight: float32 [3, 3, 3, 64, 128], replicated
The draws below stay inside these ranges and needn't reach their ends.
All inputs are finite; a program needn't handle non-finite values.
Results may differ from the reference program's by a relative error of at most 0.0034.
Values may be sent and summed in bfloat16 or wider, within the bound.
No kernel may reach another device: no remote copies, remote signals or barrier semaphores. Data moves between devices by JAX's collectives and lax.ppermute only.
A program may use at most 32 MiB of HBM per device.

```python
import math
import jax
import jax.numpy as jnp
from jax import lax

CIN = 64
COUT = 128
ROWS_OUT = 4
WO = 64
SAMPLES = 16
DEPTH_OUT = 64
DEPTH = 128
HEIGHT = 8


def block_scale(key, dims, split, low, largest):
    loudness = 1.0
    for position, blocks in split:
        steps = jax.random.uniform(jax.random.fold_in(jax.random.fold_in(key, 6), position), (blocks,), jnp.float32, low / len(split), largest / len(split))
        loudness = loudness * jnp.repeat(jnp.exp(steps), dims[position] // blocks).reshape((-1,) + (1,) * (len(dims) - 1 - position))
    return loudness


def centred(stream_key, shape, width, reach, cuts=(), dtype=jnp.bfloat16):
    loudness = block_scale(stream_key, shape, cuts, -0.22, 0.18) if cuts else 1.0
    drawn = jax.random.normal(stream_key, shape, jnp.float32) * width * loudness
    return jnp.minimum(jnp.maximum(drawn, -reach), reach).astype(dtype)


def setup_inputs(seed: int = 0) -> dict:
    seeds = jax.random.split(jax.random.key(seed), 4)
    volume = centred(seeds[0], (SAMPLES, DEPTH, HEIGHT, WO, 2 * CIN), 1.0, 6.0, ((0, 16), (1, 64)))
    weight = centred(seeds[1], (3, 3, 3, CIN, COUT), (27 * CIN) ** -0.5, 0.15625)
    cotangent = centred(seeds[2], (SAMPLES, DEPTH_OUT, ROWS_OUT, WO, COUT), 1.0, 6.0, ((0, 16), (1, 64)))
    return {"volume": volume, "weight": weight, "cotangent": cotangent}


def convolve(field, kernel):
    return lax.conv_general_dilated(field, kernel, (2, 2, 2), ((1, 1), (1, 1), (1, 1)), dimension_numbers=('NDHWC', 'DHWIO', 'NDHWC'), precision=lax.Precision.HIGHEST)

def reference(volume, weight, cotangent):
    kernel = weight.astype(jnp.float32)

    def one_sample(carry, pair_in):
        sample, grad_out = pair_in
        field = sample.reshape(DEPTH, HEIGHT, 2 * WO, CIN)[None].astype(jnp.float32)
        result, pull = jax.vjp(convolve, field, kernel)
        grad_field, grad_kernel = pull(grad_out[None].astype(jnp.float32))
        paired = grad_field[0].reshape(DEPTH, HEIGHT, WO, 2 * CIN).astype(jnp.bfloat16)
        return (carry + grad_kernel, (result[0].astype(jnp.bfloat16), paired))
    start = jnp.zeros((3, 3, 3, CIN, COUT), jnp.float32)
    total, (output, grad_volume) = lax.scan(one_sample, start, (volume, cotangent))
    grad_weight = total * (1.0 / math.sqrt(SAMPLES * DEPTH_OUT * ROWS_OUT * WO))
    return (output, grad_volume, grad_weight)
```

```python
import math

import jax
import jax.numpy as jnp
from jax import lax
from jax.experimental import pallas as pl
from jax.experimental.pallas import tpu as pltpu
from jax.sharding import PartitionSpec as P

DP = ("x", "zh")
SPACE = ("y", "zl", "c")
PLANE = ("x", "y", "c")
SIZES = (4, 4, 4, 8, 2)
VMEM_BYTES = 16 << 20


def passed_along(value, axes, steps):
    count = math.prod(lax.axis_size(axis) for axis in axes)
    first, last = (max(0, -steps), min(count, count - steps))
    return lax.ppermute(value, axes, [(source, source + steps) for source in range(first, last)])


def exchange(value, axes):
    return lax.all_to_all(value, axes, 0, 0, tiled=True)


def with_next_pair(cells, pairs):
    wide = cells.astype(jnp.float32)
    rows = wide.shape[0]
    row = lax.broadcasted_iota(jnp.int32, wide.shape, 0)
    ahead = jnp.where(row % pairs == pairs - 1, 0.0, pltpu.roll(wide, rows - 1, 0))
    return jnp.concatenate([cells, ahead.astype(jnp.bfloat16)], axis=1)


def from_previous_pair(wide, pairs):
    row = lax.broadcasted_iota(jnp.int32, wide.shape, 0)
    return jnp.where(row % pairs == 0, 0.0, pltpu.roll(wide, 1, 0))


def plane_rows(plane, rows_out):
    even = jnp.concatenate([plane[2 * b] for b in range(rows_out)], axis=0)
    odd = jnp.concatenate([plane[2 * b + 1] for b in range(rows_out)], axis=0)
    return even, odd


def tap_weight(weight, depth_tap, height_tap):
    taps = weight[depth_tap, height_tap]
    pair = jnp.concatenate([taps[1], taps[2]], axis=0)
    left = jnp.concatenate([jnp.zeros_like(taps[0]), taps[0]], axis=0)
    return jnp.concatenate([pair, left], axis=1)


def forward_dot(rows, weight):
    return lax.dot_general(
        rows, weight, (((1,), (0,)), ((), ())), preferred_element_type=jnp.float32
    )


def backward_dot(rows, weight):
    return lax.dot_general(
        rows, weight, (((1,), (1,)), ((), ())), preferred_element_type=jnp.float32
    )


def kernel_dot(rows, grads):
    return lax.dot_general(
        rows, grads, (((0,), (0,)), ((), ())), preferred_element_type=jnp.float32
    )


def store_kernel_terms(terms_ref, depth_tap, plane, grads, rows_out, pairs, cin, cout):
    even, odd = plane_rows(plane, rows_out)
    kept = (rows_out - 1) * pairs
    products = (
        kernel_dot(odd[:kept], grads[pairs:]),
        kernel_dot(even, grads),
        kernel_dot(odd, grads),
    )
    for height_tap in range(3):
        product = products[height_tap]
        base = (depth_tap * 3 + height_tap) * 3 * cin
        terms_ref[base : base + cin] = product[cin:, cout:]
        terms_ref[base + cin : base + 3 * cin] = product[:, :cout]


def forward_terms(plane, weight, depth_tap, rows_out, pairs):
    even, odd = plane_rows(plane, rows_out)
    lifted = jnp.concatenate([jnp.zeros_like(odd[:pairs]), odd[: (rows_out - 1) * pairs]], axis=0)
    return (
        forward_dot(lifted, tap_weight(weight, depth_tap, 0))
        + forward_dot(even, tap_weight(weight, depth_tap, 1))
        + forward_dot(odd, tap_weight(weight, depth_tap, 2))
    )


def backward_terms(grads, weight, depth_tap, pairs):
    raised = jnp.concatenate([grads[pairs:], jnp.zeros_like(grads[:pairs])], axis=0)
    even = backward_dot(grads, tap_weight(weight, depth_tap, 1))
    odd = backward_dot(grads, tap_weight(weight, depth_tap, 2)) + backward_dot(
        raised, tap_weight(weight, depth_tap, 0)
    )
    return even, odd


def own_kernel(local_ref, grads_ref, weight_ref, terms_ref, forward_ref, first_ref, second_ref):
    rows_out, pairs, cout = grads_ref.shape
    cin = weight_ref.shape[3]
    grads = with_next_pair(grads_ref[...].reshape(rows_out * pairs, cout), pairs)
    for depth_tap in (1, 2):
        plane = local_ref[depth_tap - 1]
        store_kernel_terms(terms_ref, depth_tap - 1, plane, grads, rows_out, pairs, cin, cout)
    forward_ref[...] = forward_terms(local_ref[0], weight_ref, 1, rows_out, pairs) + forward_terms(
        local_ref[1], weight_ref, 2, rows_out, pairs
    )
    even, odd = backward_terms(grads, weight_ref, 1, pairs)
    for b in range(rows_out):
        first_ref[2 * b] = even[b * pairs : (b + 1) * pairs].astype(jnp.bfloat16)
        first_ref[2 * b + 1] = odd[b * pairs : (b + 1) * pairs].astype(jnp.bfloat16)
    even, odd = backward_terms(grads, weight_ref, 2, pairs)
    second_ref[0] = even
    second_ref[1] = odd


def joined_kernel(local_ref, later_ref, terms_ref, chunks_ref, scratch_ref):
    rows_out, pairs, cout = later_ref.shape
    cin = local_ref.shape[3] // 2
    count, rows, _ = chunks_ref.shape
    total = 27 * cin
    step = total // count
    later = with_next_pair(later_ref[...].reshape(rows_out * pairs, cout), pairs)
    store_kernel_terms(scratch_ref, 0, local_ref[1], later, rows_out, pairs, cin, cout)
    scratch_ref[9 * cin : total] = terms_ref[...]
    scratch_ref[total:] = jnp.zeros((scratch_ref.shape[0] - total, cout), jnp.float32)
    for index in range(count):
        chunks_ref[index] = scratch_ref[index * step : index * step + rows].astype(chunks_ref.dtype)


def finish_kernel(
    rim_ref, later_ref, weight_ref, forward_ref, first_ref, second_ref, output_ref, grad_ref
):
    rows_out, pairs, cout = later_ref.shape
    later = with_next_pair(later_ref[...].reshape(rows_out * pairs, cout), pairs)
    total = forward_ref[...] + forward_terms(rim_ref[0], weight_ref, 0, rows_out, pairs)
    result = total[:, :cout] + from_previous_pair(total[:, cout:], pairs)
    output_ref[...] = result.astype(jnp.bfloat16).reshape(output_ref.shape)
    even, odd = backward_terms(later, weight_ref, 0, pairs)
    even = (even + second_ref[0]).astype(jnp.bfloat16)
    odd = (odd + second_ref[1]).astype(jnp.bfloat16)
    grad_ref[0] = first_ref[...]
    for b in range(rows_out):
        grad_ref[1, 2 * b] = even[b * pairs : (b + 1) * pairs]
        grad_ref[1, 2 * b + 1] = odd[b * pairs : (b + 1) * pairs]


def spread_kernel(step, factor, chunks_ref, grad_ref):
    for index in range(chunks_ref.shape[0]):
        block = chunks_ref[index].astype(jnp.float32)[:step]
        grad_ref[index * step : (index + 1) * step] = block * factor


def shards(volume, weight, cotangent):
    local = volume[0]
    grads = cotangent[0, 0]
    rows_out, pairs, cout = grads.shape
    cin = weight.shape[3]
    total = 27 * cin
    cells = rows_out * pairs
    count = math.prod(lax.axis_size(axis) for axis in PLANE)
    step = total // count
    rows = -(-step // 8) * 8
    devices = math.prod(lax.axis_size(axis) for axis in DP + SPACE)
    factor = 1.0 / math.sqrt(devices * cells)

    later = passed_along(grads, SPACE, -1)
    rim = passed_along(local[1:2], SPACE, 1)
    terms, forward, first, second = pl.pallas_call(
        own_kernel,
        out_shape=(
            jax.ShapeDtypeStruct((18 * cin, cout), jnp.float32),
            jax.ShapeDtypeStruct((cells, 2 * cout), jnp.float32),
            jax.ShapeDtypeStruct((2 * rows_out, pairs, 2 * cin), jnp.bfloat16),
            jax.ShapeDtypeStruct((2, cells, 2 * cin), jnp.float32),
        ),
        cost_estimate=pl.CostEstimate(flops=300_000_000, bytes_accessed=2_000_000, transcendentals=0),
        compiler_params=pltpu.CompilerParams(vmem_limit_bytes=VMEM_BYTES),
        name="own",
    )(local, grads, weight)
    chunks = pl.pallas_call(
        joined_kernel,
        out_shape=jax.ShapeDtypeStruct((count, rows, cout), jnp.bfloat16),
        scratch_shapes=[pltpu.VMEM((total + 8, cout), jnp.float32)],
        cost_estimate=pl.CostEstimate(flops=60_000_000, bytes_accessed=1_000_000, transcendentals=0),
        compiler_params=pltpu.CompilerParams(vmem_limit_bytes=VMEM_BYTES),
        name="joined",
    )(local, later, terms)

    piece = jnp.sum(exchange(chunks, PLANE).astype(jnp.float32), axis=0)
    for axis in ("zl", "zh"):
        copies = jnp.broadcast_to(piece[None], (lax.axis_size(axis), rows, cout))
        piece = jnp.sum(exchange(copies, (axis,)), axis=0)
    copies = jnp.broadcast_to(piece.astype(jnp.bfloat16)[None], (count, rows, cout))
    gathered = exchange(copies, PLANE)

    output, grad_volume = pl.pallas_call(
        finish_kernel,
        out_shape=(
            jax.ShapeDtypeStruct((rows_out, pairs, cout), jnp.bfloat16),
            jax.ShapeDtypeStruct((2, 2 * rows_out, pairs, 2 * cin), jnp.bfloat16),
        ),
        cost_estimate=pl.CostEstimate(flops=100_000_000, bytes_accessed=1_000_000, transcendentals=0),
        compiler_params=pltpu.CompilerParams(vmem_limit_bytes=VMEM_BYTES),
        name="finish",
    )(rim, later, weight, forward, first, second)
    grad_weight = pl.pallas_call(
        lambda chunks_ref, grad_ref: spread_kernel(step, factor, chunks_ref, grad_ref),
        out_shape=jax.ShapeDtypeStruct((total, cout), jnp.float32),
        compiler_params=pltpu.CompilerParams(vmem_limit_bytes=VMEM_BYTES),
        name="spread_out",
    )(gathered)
    return (output[None, None], grad_volume[None], grad_weight.reshape(weight.shape))


def solution(mesh):
    fine = jax.sharding.Mesh(mesh.devices.reshape(SIZES), DP + SPACE)
    split = P(DP, SPACE, None, None, None)
    return jax.shard_map(
        shards,
        mesh=fine,
        in_specs=(split, P(), split),
        out_specs=(split, split, P()),
        check_vma=False,
    )
```

```python
import math

import jax
import jax.numpy as jnp
from jax import lax
from jax.experimental import pallas as pl
from jax.experimental.pallas import tpu as pltpu
from jax.sharding import PartitionSpec as P

DP = ("x", "zh")
SPACE = ("y", "zn", "ze", "c")
SLAB = ("x", "y", "ze", "c")
SIZES = (4, 4, 4, 4, 2, 2)
VMEM_BYTES = 16 << 20


def passed_along(value, axes, steps):
    count = math.prod(lax.axis_size(axis) for axis in axes)
    first, last = (max(0, -steps), min(count, count - steps))
    return lax.ppermute(value, axes, [(source, source + steps) for source in range(first, last)])


def exchange(value, axes):
    return lax.all_to_all(value, axes, 0, 0, tiled=True)


def summed_over(piece, axis):
    copies = jnp.broadcast_to(piece[None], (lax.axis_size(axis), *piece.shape))
    return jnp.sum(exchange(copies, (axis,)), axis=0)


def with_next_pair(cells, pairs):
    wide = cells.astype(jnp.float32)
    rows = wide.shape[0]
    row = lax.broadcasted_iota(jnp.int32, wide.shape, 0)
    ahead = jnp.where(row % pairs == pairs - 1, 0.0, pltpu.roll(wide, rows - 1, 0))
    return jnp.concatenate([cells, ahead.astype(jnp.bfloat16)], axis=1)


def from_previous_pair(wide, pairs):
    row = lax.broadcasted_iota(jnp.int32, wide.shape, 0)
    return jnp.where(row % pairs == 0, 0.0, pltpu.roll(wide, 1, 0))


def plane_rows(plane, rows_out):
    even = jnp.concatenate([plane[2 * b] for b in range(rows_out)], axis=0)
    odd = jnp.concatenate([plane[2 * b + 1] for b in range(rows_out)], axis=0)
    return even, odd


def tap_weight(weight, depth_tap, height_tap):
    taps = weight[depth_tap, height_tap]
    pair = jnp.concatenate([taps[1], taps[2]], axis=0)
    left = jnp.concatenate([jnp.zeros_like(taps[0]), taps[0]], axis=0)
    return jnp.concatenate([pair, left], axis=1)


def forward_dot(rows, weight):
    return lax.dot_general(
        rows, weight, (((1,), (0,)), ((), ())), preferred_element_type=jnp.float32
    )


def backward_dot(rows, weight):
    return lax.dot_general(
        rows, weight, (((1,), (1,)), ((), ())), preferred_element_type=jnp.float32
    )


def kernel_dot(rows, grads):
    return lax.dot_general(
        rows, grads, (((0,), (0,)), ((), ())), preferred_element_type=jnp.float32
    )


def store_kernel_terms(terms_ref, depth_tap, plane, grads, rows_out, pairs, cin, cout):
    even, odd = plane_rows(plane, rows_out)
    kept = (rows_out - 1) * pairs
    products = (
        kernel_dot(odd[:kept], grads[pairs:]),
        kernel_dot(even, grads),
        kernel_dot(odd, grads),
    )
    for height_tap in range(3):
        product = products[height_tap]
        base = (depth_tap * 3 + height_tap) * 3 * cin
        terms_ref[base : base + cin] = product[cin:, cout:]
        terms_ref[base + cin : base + 3 * cin] = product[:, :cout]


def forward_terms(plane, weight, depth_tap, rows_out, pairs):
    even, odd = plane_rows(plane, rows_out)
    lifted = jnp.concatenate([jnp.zeros_like(odd[:pairs]), odd[: (rows_out - 1) * pairs]], axis=0)
    return (
        forward_dot(lifted, tap_weight(weight, depth_tap, 0))
        + forward_dot(even, tap_weight(weight, depth_tap, 1))
        + forward_dot(odd, tap_weight(weight, depth_tap, 2))
    )


def backward_terms(grads, weight, depth_tap, pairs):
    raised = jnp.concatenate([grads[pairs:], jnp.zeros_like(grads[:pairs])], axis=0)
    even = backward_dot(grads, tap_weight(weight, depth_tap, 1))
    odd = backward_dot(grads, tap_weight(weight, depth_tap, 2)) + backward_dot(
        raised, tap_weight(weight, depth_tap, 0)
    )
    return even, odd


def own_kernel(local_ref, grads_ref, weight_ref, terms_ref, forward_ref, first_ref, second_ref):
    rows_out, pairs, cout = grads_ref.shape
    cin = weight_ref.shape[3]
    grads = with_next_pair(grads_ref[...].reshape(rows_out * pairs, cout), pairs)
    for depth_tap in (1, 2):
        plane = local_ref[depth_tap - 1]
        store_kernel_terms(terms_ref, depth_tap - 1, plane, grads, rows_out, pairs, cin, cout)
    forward_ref[...] = forward_terms(local_ref[0], weight_ref, 1, rows_out, pairs) + forward_terms(
        local_ref[1], weight_ref, 2, rows_out, pairs
    )
    even, odd = backward_terms(grads, weight_ref, 1, pairs)
    for b in range(rows_out):
        first_ref[2 * b] = even[b * pairs : (b + 1) * pairs].astype(jnp.bfloat16)
        first_ref[2 * b + 1] = odd[b * pairs : (b + 1) * pairs].astype(jnp.bfloat16)
    even, odd = backward_terms(grads, weight_ref, 2, pairs)
    second_ref[0] = even
    second_ref[1] = odd


def joined_kernel(local_ref, later_ref, terms_ref, chunks_ref, scratch_ref):
    rows_out, pairs, cout = later_ref.shape
    cin = local_ref.shape[3] // 2
    count, rows, _ = chunks_ref.shape
    total = 27 * cin
    step = total // count
    later = with_next_pair(later_ref[...].reshape(rows_out * pairs, cout), pairs)
    store_kernel_terms(scratch_ref, 0, local_ref[1], later, rows_out, pairs, cin, cout)
    scratch_ref[9 * cin : total] = terms_ref[...]
    scratch_ref[total:] = jnp.zeros((scratch_ref.shape[0] - total, cout), jnp.float32)
    for index in range(count):
        chunks_ref[index] = scratch_ref[index * step : index * step + rows].astype(chunks_ref.dtype)


def finish_kernel(
    rim_ref, later_ref, weight_ref, forward_ref, first_ref, second_ref, output_ref, grad_ref
):
    rows_out, pairs, cout = later_ref.shape
    later = with_next_pair(later_ref[...].reshape(rows_out * pairs, cout), pairs)
    total = forward_ref[...] + forward_terms(rim_ref[0], weight_ref, 0, rows_out, pairs)
    result = total[:, :cout] + from_previous_pair(total[:, cout:], pairs)
    output_ref[...] = result.astype(jnp.bfloat16).reshape(output_ref.shape)
    even, odd = backward_terms(later, weight_ref, 0, pairs)
    even = (even + second_ref[0]).astype(jnp.bfloat16)
    odd = (odd + second_ref[1]).astype(jnp.bfloat16)
    grad_ref[0] = first_ref[...]
    for b in range(rows_out):
        grad_ref[1, 2 * b] = even[b * pairs : (b + 1) * pairs]
        grad_ref[1, 2 * b + 1] = odd[b * pairs : (b + 1) * pairs]


def spread_kernel(step, factor, chunks_ref, grad_ref):
    for index in range(chunks_ref.shape[0]):
        block = chunks_ref[index].astype(jnp.float32)[:step]
        grad_ref[index * step : (index + 1) * step] = block * factor


def shards(volume, weight, cotangent):
    local = volume[0]
    grads = cotangent[0, 0]
    rows_out, pairs, cout = grads.shape
    cin = weight.shape[3]
    total = 27 * cin
    cells = rows_out * pairs
    count = math.prod(lax.axis_size(axis) for axis in SLAB)
    step = total // count
    rows = -(-step // 8) * 8
    devices = math.prod(lax.axis_size(axis) for axis in DP + SPACE)
    factor = 1.0 / math.sqrt(devices * cells)

    later = passed_along(grads, SPACE, -1)
    terms, forward, first, second = pl.pallas_call(
        own_kernel,
        out_shape=(
            jax.ShapeDtypeStruct((18 * cin, cout), jnp.float32),
            jax.ShapeDtypeStruct((cells, 2 * cout), jnp.float32),
            jax.ShapeDtypeStruct((2 * rows_out, pairs, 2 * cin), jnp.bfloat16),
            jax.ShapeDtypeStruct((2, cells, 2 * cin), jnp.float32),
        ),
        cost_estimate=pl.CostEstimate(flops=300_000_000, bytes_accessed=2_000_000, transcendentals=0),
        compiler_params=pltpu.CompilerParams(vmem_limit_bytes=VMEM_BYTES),
        name="own",
    )(local, grads, weight)
    chunks = pl.pallas_call(
        joined_kernel,
        out_shape=jax.ShapeDtypeStruct((count, rows, cout), jnp.bfloat16),
        scratch_shapes=[pltpu.VMEM((total + 8, cout), jnp.float32)],
        cost_estimate=pl.CostEstimate(flops=60_000_000, bytes_accessed=1_000_000, transcendentals=0),
        compiler_params=pltpu.CompilerParams(vmem_limit_bytes=VMEM_BYTES),
        name="joined",
    )(local, later, terms)

    piece = jnp.sum(exchange(chunks, SLAB).astype(jnp.float32), axis=0)
    piece = summed_over(piece, "zn")
    piece, plane = lax.optimization_barrier((piece, local[1:2]))
    rim = passed_along(plane, SPACE, 1)
    piece = summed_over(piece, "zh")

    output, grad_volume = pl.pallas_call(
        finish_kernel,
        out_shape=(
            jax.ShapeDtypeStruct((rows_out, pairs, cout), jnp.bfloat16),
            jax.ShapeDtypeStruct((2, 2 * rows_out, pairs, 2 * cin), jnp.bfloat16),
        ),
        cost_estimate=pl.CostEstimate(flops=100_000_000, bytes_accessed=1_000_000, transcendentals=0),
        compiler_params=pltpu.CompilerParams(vmem_limit_bytes=VMEM_BYTES),
        name="finish",
    )(rim, later, weight, forward, first, second)
    piece, output, grad_volume = lax.optimization_barrier((piece, output, grad_volume))
    copies = jnp.broadcast_to(piece.astype(jnp.bfloat16)[None], (count, rows, cout))
    gathered = exchange(copies, SLAB)
    grad_weight = pl.pallas_call(
        lambda chunks_ref, grad_ref: spread_kernel(step, factor, chunks_ref, grad_ref),
        out_shape=jax.ShapeDtypeStruct((total, cout), jnp.float32),
        compiler_params=pltpu.CompilerParams(vmem_limit_bytes=VMEM_BYTES),
        name="spread_out",
    )(gathered)
    return (output[None, None], grad_volume[None], grad_weight.reshape(weight.shape))


def solution(mesh):
    fine = jax.sharding.Mesh(mesh.devices.reshape(SIZES), DP + SPACE)
    split = P(DP, SPACE, None, None, None)
    return jax.shard_map(
        shards,
        mesh=fine,
        in_specs=(split, P(), split),
        out_specs=(split, split, P()),
        check_vma=False,
    )
```

```python
import math

import jax
import jax.numpy as jnp
from jax import lax
from jax.experimental import pallas as pl
from jax.experimental.pallas import tpu as pltpu
from jax.sharding import PartitionSpec as P

DP = ("x", "zh")
SPACE = ("y", "zn", "ze", "c")
SLAB = ("x", "y", "ze", "c")
SIZES = (4, 4, 4, 4, 2, 2)
VMEM_BYTES = 16 << 20


def passed_along(value, axes, steps):
    count = math.prod(lax.axis_size(axis) for axis in axes)
    first, last = (max(0, -steps), min(count, count - steps))
    return lax.ppermute(value, axes, [(source, source + steps) for source in range(first, last)])


def exchange(value, axes):
    return lax.all_to_all(value, axes, 0, 0, tiled=True)


def swapped_sum(piece, axis, distance):
    count = lax.axis_size(axis)
    pairs = [(source, source ^ distance) for source in range(count)]
    return piece + lax.ppermute(piece, axis, pairs)


def with_next_pair(cells, pairs):
    wide = cells.astype(jnp.float32)
    rows = wide.shape[0]
    row = lax.broadcasted_iota(jnp.int32, wide.shape, 0)
    ahead = jnp.where(row % pairs == pairs - 1, 0.0, pltpu.roll(wide, rows - 1, 0))
    return jnp.concatenate([cells, ahead.astype(jnp.bfloat16)], axis=1)


def from_previous_pair(wide, pairs):
    row = lax.broadcasted_iota(jnp.int32, wide.shape, 0)
    return jnp.where(row % pairs == 0, 0.0, pltpu.roll(wide, 1, 0))


def plane_rows(plane, rows_out):
    even = jnp.concatenate([plane[2 * b] for b in range(rows_out)], axis=0)
    odd = jnp.concatenate([plane[2 * b + 1] for b in range(rows_out)], axis=0)
    return even, odd


def tap_weight(weight, depth_tap, height_tap):
    taps = weight[depth_tap, height_tap]
    pair = jnp.concatenate([taps[1], taps[2]], axis=0)
    left = jnp.concatenate([jnp.zeros_like(taps[0]), taps[0]], axis=0)
    return jnp.concatenate([pair, left], axis=1)


def forward_dot(rows, weight):
    return lax.dot_general(
        rows, weight, (((1,), (0,)), ((), ())), preferred_element_type=jnp.float32
    )


def backward_dot(rows, weight):
    return lax.dot_general(
        rows, weight, (((1,), (1,)), ((), ())), preferred_element_type=jnp.float32
    )


def kernel_dot(rows, grads):
    return lax.dot_general(
        rows, grads, (((0,), (0,)), ((), ())), preferred_element_type=jnp.float32
    )


def store_kernel_terms(terms_ref, depth_tap, plane, grads, rows_out, pairs, cin, cout):
    even, odd = plane_rows(plane, rows_out)
    kept = (rows_out - 1) * pairs
    products = (
        kernel_dot(odd[:kept], grads[pairs:]),
        kernel_dot(even, grads),
        kernel_dot(odd, grads),
    )
    for height_tap in range(3):
        product = products[height_tap]
        base = (depth_tap * 3 + height_tap) * 3 * cin
        terms_ref[base : base + cin] = product[cin:, cout:]
        terms_ref[base + cin : base + 3 * cin] = product[:, :cout]


def forward_terms(plane, weight, depth_tap, rows_out, pairs):
    even, odd = plane_rows(plane, rows_out)
    lifted = jnp.concatenate([jnp.zeros_like(odd[:pairs]), odd[: (rows_out - 1) * pairs]], axis=0)
    return (
        forward_dot(lifted, tap_weight(weight, depth_tap, 0))
        + forward_dot(even, tap_weight(weight, depth_tap, 1))
        + forward_dot(odd, tap_weight(weight, depth_tap, 2))
    )


def backward_terms(grads, weight, depth_tap, pairs):
    raised = jnp.concatenate([grads[pairs:], jnp.zeros_like(grads[:pairs])], axis=0)
    even = backward_dot(grads, tap_weight(weight, depth_tap, 1))
    odd = backward_dot(grads, tap_weight(weight, depth_tap, 2)) + backward_dot(
        raised, tap_weight(weight, depth_tap, 0)
    )
    return even, odd


def own_kernel(local_ref, grads_ref, weight_ref, terms_ref, forward_ref, first_ref, second_ref):
    rows_out, pairs, cout = grads_ref.shape
    cin = weight_ref.shape[3]
    grads = with_next_pair(grads_ref[...].reshape(rows_out * pairs, cout), pairs)
    for depth_tap in (1, 2):
        plane = local_ref[depth_tap - 1]
        store_kernel_terms(terms_ref, depth_tap - 1, plane, grads, rows_out, pairs, cin, cout)
    forward_ref[...] = forward_terms(local_ref[0], weight_ref, 1, rows_out, pairs) + forward_terms(
        local_ref[1], weight_ref, 2, rows_out, pairs
    )
    even, odd = backward_terms(grads, weight_ref, 1, pairs)
    for b in range(rows_out):
        first_ref[2 * b] = even[b * pairs : (b + 1) * pairs].astype(jnp.bfloat16)
        first_ref[2 * b + 1] = odd[b * pairs : (b + 1) * pairs].astype(jnp.bfloat16)
    even, odd = backward_terms(grads, weight_ref, 2, pairs)
    second_ref[0] = even
    second_ref[1] = odd


def joined_kernel(local_ref, later_ref, terms_ref, chunks_ref, scratch_ref):
    rows_out, pairs, cout = later_ref.shape
    cin = local_ref.shape[3] // 2
    count, rows, _ = chunks_ref.shape
    total = 27 * cin
    step = total // count
    later = with_next_pair(later_ref[...].reshape(rows_out * pairs, cout), pairs)
    store_kernel_terms(scratch_ref, 0, local_ref[1], later, rows_out, pairs, cin, cout)
    scratch_ref[9 * cin : total] = terms_ref[...]
    scratch_ref[total:] = jnp.zeros((scratch_ref.shape[0] - total, cout), jnp.float32)
    for index in range(count):
        chunks_ref[index] = scratch_ref[index * step : index * step + rows].astype(chunks_ref.dtype)


def finish_kernel(
    rim_ref, later_ref, weight_ref, forward_ref, first_ref, second_ref, output_ref, grad_ref
):
    rows_out, pairs, cout = later_ref.shape
    later = with_next_pair(later_ref[...].reshape(rows_out * pairs, cout), pairs)
    total = forward_ref[...] + forward_terms(rim_ref[0], weight_ref, 0, rows_out, pairs)
    result = total[:, :cout] + from_previous_pair(total[:, cout:], pairs)
    output_ref[...] = result.astype(jnp.bfloat16).reshape(output_ref.shape)
    even, odd = backward_terms(later, weight_ref, 0, pairs)
    even = (even + second_ref[0]).astype(jnp.bfloat16)
    odd = (odd + second_ref[1]).astype(jnp.bfloat16)
    grad_ref[0] = first_ref[...]
    for b in range(rows_out):
        grad_ref[1, 2 * b] = even[b * pairs : (b + 1) * pairs]
        grad_ref[1, 2 * b + 1] = odd[b * pairs : (b + 1) * pairs]


def spread_kernel(step, factor, chunks_ref, grad_ref):
    for index in range(chunks_ref.shape[0]):
        block = chunks_ref[index].astype(jnp.float32)[:step]
        grad_ref[index * step : (index + 1) * step] = block * factor


def shards(volume, weight, cotangent):
    local = volume[0]
    grads = cotangent[0, 0]
    rows_out, pairs, cout = grads.shape
    cin = weight.shape[3]
    total = 27 * cin
    cells = rows_out * pairs
    count = math.prod(lax.axis_size(axis) for axis in SLAB)
    step = total // count
    rows = -(-step // 8) * 8
    devices = math.prod(lax.axis_size(axis) for axis in DP + SPACE)
    factor = 1.0 / math.sqrt(devices * cells)

    later = passed_along(grads, SPACE, -1)
    rim = passed_along(local[1:2], SPACE, 1)
    terms, forward, first, second = pl.pallas_call(
        own_kernel,
        out_shape=(
            jax.ShapeDtypeStruct((18 * cin, cout), jnp.float32),
            jax.ShapeDtypeStruct((cells, 2 * cout), jnp.float32),
            jax.ShapeDtypeStruct((2 * rows_out, pairs, 2 * cin), jnp.bfloat16),
            jax.ShapeDtypeStruct((2, cells, 2 * cin), jnp.float32),
        ),
        cost_estimate=pl.CostEstimate(flops=300_000_000, bytes_accessed=2_000_000, transcendentals=0),
        compiler_params=pltpu.CompilerParams(vmem_limit_bytes=VMEM_BYTES),
        name="own",
    )(local, grads, weight)
    chunks = pl.pallas_call(
        joined_kernel,
        out_shape=jax.ShapeDtypeStruct((count, rows, cout), jnp.bfloat16),
        scratch_shapes=[pltpu.VMEM((total + 8, cout), jnp.float32)],
        cost_estimate=pl.CostEstimate(flops=60_000_000, bytes_accessed=1_000_000, transcendentals=0),
        compiler_params=pltpu.CompilerParams(vmem_limit_bytes=VMEM_BYTES),
        name="joined",
    )(local, later, terms)

    piece = jnp.sum(exchange(chunks, SLAB).astype(jnp.float32), axis=0)
    for axis in ("zn", "zh"):
        for bit in range(lax.axis_size(axis).bit_length() - 1):
            piece = swapped_sum(piece, axis, 1 << bit)
        if axis == "zn":
            piece, rim = lax.optimization_barrier((piece, rim))

    output, grad_volume = pl.pallas_call(
        finish_kernel,
        out_shape=(
            jax.ShapeDtypeStruct((rows_out, pairs, cout), jnp.bfloat16),
            jax.ShapeDtypeStruct((2, 2 * rows_out, pairs, 2 * cin), jnp.bfloat16),
        ),
        cost_estimate=pl.CostEstimate(flops=100_000_000, bytes_accessed=1_000_000, transcendentals=0),
        compiler_params=pltpu.CompilerParams(vmem_limit_bytes=VMEM_BYTES),
        name="finish",
    )(rim, later, weight, forward, first, second)
    copies = jnp.broadcast_to(piece.astype(jnp.bfloat16)[None], (count, rows, cout))
    gathered = exchange(copies, SLAB)
    grad_weight = pl.pallas_call(
        lambda chunks_ref, grad_ref: spread_kernel(step, factor, chunks_ref, grad_ref),
        out_shape=jax.ShapeDtypeStruct((total, cout), jnp.float32),
        compiler_params=pltpu.CompilerParams(vmem_limit_bytes=VMEM_BYTES),
        name="spread_out",
    )(gathered)
    return (output[None, None], grad_volume[None], grad_weight.reshape(weight.shape))


def solution(mesh):
    fine = jax.sharding.Mesh(mesh.devices.reshape(SIZES), DP + SPACE)
    split = P(DP, SPACE, None, None, None)
    return jax.shard_map(
        shards,
        mesh=fine,
        in_specs=(split, P(), split),
        out_specs=(split, split, P()),
        check_vma=False,
    )
```

```python
import math

import jax
import jax.numpy as jnp
from jax import lax
from jax.experimental import pallas as pl
from jax.experimental.pallas import tpu as pltpu
from jax.sharding import PartitionSpec as P

DP = ("x", "zh")
SPACE = ("y", "zn", "ze", "c")
SLAB = ("x", "y", "ze", "c")
LINE = ("zh", "zn")
SIZES = (4, 4, 4, 4, 2, 2)
VMEM_BYTES = 16 << 20


def passed_along(value, axes, steps):
    count = math.prod(lax.axis_size(axis) for axis in axes)
    first, last = (max(0, -steps), min(count, count - steps))
    return lax.ppermute(value, axes, [(source, source + steps) for source in range(first, last)])


def exchange(value, axes):
    return lax.all_to_all(value, axes, 0, 0, tiled=True)


def with_next_pair(cells, pairs):
    wide = cells.astype(jnp.float32)
    rows = wide.shape[0]
    row = lax.broadcasted_iota(jnp.int32, wide.shape, 0)
    ahead = jnp.where(row % pairs == pairs - 1, 0.0, pltpu.roll(wide, rows - 1, 0))
    return jnp.concatenate([cells, ahead.astype(jnp.bfloat16)], axis=1)


def from_previous_pair(wide, pairs):
    row = lax.broadcasted_iota(jnp.int32, wide.shape, 0)
    return jnp.where(row % pairs == 0, 0.0, pltpu.roll(wide, 1, 0))


def plane_rows(plane, rows_out):
    even = jnp.concatenate([plane[2 * b] for b in range(rows_out)], axis=0)
    odd = jnp.concatenate([plane[2 * b + 1] for b in range(rows_out)], axis=0)
    return even, odd


def tap_weight(weight, depth_tap, height_tap):
    taps = weight[depth_tap, height_tap]
    pair = jnp.concatenate([taps[1], taps[2]], axis=0)
    left = jnp.concatenate([jnp.zeros_like(taps[0]), taps[0]], axis=0)
    return jnp.concatenate([pair, left], axis=1)


def forward_dot(rows, weight):
    return lax.dot_general(
        rows, weight, (((1,), (0,)), ((), ())), preferred_element_type=jnp.float32
    )


def backward_dot(rows, weight):
    return lax.dot_general(
        rows, weight, (((1,), (1,)), ((), ())), preferred_element_type=jnp.float32
    )


def kernel_dot(rows, grads):
    return lax.dot_general(
        rows, grads, (((0,), (0,)), ((), ())), preferred_element_type=jnp.float32
    )


def store_kernel_terms(terms_ref, depth_tap, plane, grads, rows_out, pairs, cin, cout):
    even, odd = plane_rows(plane, rows_out)
    kept = (rows_out - 1) * pairs
    products = (
        kernel_dot(odd[:kept], grads[pairs:]),
        kernel_dot(even, grads),
        kernel_dot(odd, grads),
    )
    for height_tap in range(3):
        product = products[height_tap]
        base = (depth_tap * 3 + height_tap) * 3 * cin
        terms_ref[base : base + cin] = product[cin:, cout:]
        terms_ref[base + cin : base + 3 * cin] = product[:, :cout]


def forward_terms(plane, weight, depth_tap, rows_out, pairs):
    even, odd = plane_rows(plane, rows_out)
    lifted = jnp.concatenate([jnp.zeros_like(odd[:pairs]), odd[: (rows_out - 1) * pairs]], axis=0)
    return (
        forward_dot(lifted, tap_weight(weight, depth_tap, 0))
        + forward_dot(even, tap_weight(weight, depth_tap, 1))
        + forward_dot(odd, tap_weight(weight, depth_tap, 2))
    )


def backward_terms(grads, weight, depth_tap, pairs):
    raised = jnp.concatenate([grads[pairs:], jnp.zeros_like(grads[:pairs])], axis=0)
    even = backward_dot(grads, tap_weight(weight, depth_tap, 1))
    odd = backward_dot(grads, tap_weight(weight, depth_tap, 2)) + backward_dot(
        raised, tap_weight(weight, depth_tap, 0)
    )
    return even, odd


def own_kernel(local_ref, grads_ref, weight_ref, terms_ref, forward_ref, first_ref, second_ref):
    rows_out, pairs, cout = grads_ref.shape
    cin = weight_ref.shape[3]
    grads = with_next_pair(grads_ref[...].reshape(rows_out * pairs, cout), pairs)
    for depth_tap in (1, 2):
        plane = local_ref[depth_tap - 1]
        store_kernel_terms(terms_ref, depth_tap - 1, plane, grads, rows_out, pairs, cin, cout)
    forward_ref[...] = forward_terms(local_ref[0], weight_ref, 1, rows_out, pairs) + forward_terms(
        local_ref[1], weight_ref, 2, rows_out, pairs
    )
    even, odd = backward_terms(grads, weight_ref, 1, pairs)
    for b in range(rows_out):
        first_ref[2 * b] = even[b * pairs : (b + 1) * pairs].astype(jnp.bfloat16)
        first_ref[2 * b + 1] = odd[b * pairs : (b + 1) * pairs].astype(jnp.bfloat16)
    even, odd = backward_terms(grads, weight_ref, 2, pairs)
    second_ref[0] = even
    second_ref[1] = odd


def joined_kernel(local_ref, later_ref, terms_ref, chunks_ref, scratch_ref):
    rows_out, pairs, cout = later_ref.shape
    cin = local_ref.shape[3] // 2
    count, rows, _ = chunks_ref.shape
    total = 27 * cin
    step = total // count
    later = with_next_pair(later_ref[...].reshape(rows_out * pairs, cout), pairs)
    store_kernel_terms(scratch_ref, 0, local_ref[1], later, rows_out, pairs, cin, cout)
    scratch_ref[9 * cin : total] = terms_ref[...]
    scratch_ref[total:] = jnp.zeros((scratch_ref.shape[0] - total, cout), jnp.float32)
    for index in range(count):
        chunks_ref[index] = scratch_ref[index * step : index * step + rows].astype(chunks_ref.dtype)


def finish_kernel(
    rim_ref, later_ref, weight_ref, forward_ref, first_ref, second_ref, output_ref, grad_ref
):
    rows_out, pairs, cout = later_ref.shape
    later = with_next_pair(later_ref[...].reshape(rows_out * pairs, cout), pairs)
    total = forward_ref[...] + forward_terms(rim_ref[0], weight_ref, 0, rows_out, pairs)
    result = total[:, :cout] + from_previous_pair(total[:, cout:], pairs)
    output_ref[...] = result.astype(jnp.bfloat16).reshape(output_ref.shape)
    even, odd = backward_terms(later, weight_ref, 0, pairs)
    even = (even + second_ref[0]).astype(jnp.bfloat16)
    odd = (odd + second_ref[1]).astype(jnp.bfloat16)
    grad_ref[0] = first_ref[...]
    for b in range(rows_out):
        grad_ref[1, 2 * b] = even[b * pairs : (b + 1) * pairs]
        grad_ref[1, 2 * b + 1] = odd[b * pairs : (b + 1) * pairs]


def spread_kernel(step, factor, chunks_ref, grad_ref):
    for index in range(chunks_ref.shape[0]):
        block = chunks_ref[index].astype(jnp.float32)[:step]
        grad_ref[index * step : (index + 1) * step] = block * factor


def shards(volume, weight, cotangent):
    local = volume[0]
    grads = cotangent[0, 0]
    rows_out, pairs, cout = grads.shape
    cin = weight.shape[3]
    total = 27 * cin
    cells = rows_out * pairs
    count = math.prod(lax.axis_size(axis) for axis in SLAB)
    step = total // count
    rows = -(-step // 8) * 8
    devices = math.prod(lax.axis_size(axis) for axis in DP + SPACE)
    factor = 1.0 / math.sqrt(devices * cells)

    later = passed_along(grads, SPACE, -1)
    terms, forward, first, second = pl.pallas_call(
        own_kernel,
        out_shape=(
            jax.ShapeDtypeStruct((18 * cin, cout), jnp.float32),
            jax.ShapeDtypeStruct((cells, 2 * cout), jnp.float32),
            jax.ShapeDtypeStruct((2 * rows_out, pairs, 2 * cin), jnp.bfloat16),
            jax.ShapeDtypeStruct((2, cells, 2 * cin), jnp.float32),
        ),
        cost_estimate=pl.CostEstimate(flops=300_000_000, bytes_accessed=2_000_000, transcendentals=0),
        compiler_params=pltpu.CompilerParams(vmem_limit_bytes=VMEM_BYTES),
        name="own",
    )(local, grads, weight)
    chunks = pl.pallas_call(
        joined_kernel,
        out_shape=jax.ShapeDtypeStruct((count, rows, cout), jnp.bfloat16),
        scratch_shapes=[pltpu.VMEM((total + 8, cout), jnp.float32)],
        cost_estimate=pl.CostEstimate(flops=60_000_000, bytes_accessed=1_000_000, transcendentals=0),
        compiler_params=pltpu.CompilerParams(vmem_limit_bytes=VMEM_BYTES),
        name="joined",
    )(local, later, terms)

    piece = jnp.sum(exchange(chunks, SLAB).astype(jnp.float32), axis=0)
    piece, plane = lax.optimization_barrier((piece, local[1:2]))
    rim = passed_along(plane, SPACE, 1)
    lines = math.prod(lax.axis_size(axis) for axis in LINE)
    copies = jnp.broadcast_to(piece[None], (lines, rows, cout))
    piece = jnp.sum(exchange(copies, LINE), axis=0)

    output, grad_volume = pl.pallas_call(
        finish_kernel,
        out_shape=(
            jax.ShapeDtypeStruct((rows_out, pairs, cout), jnp.bfloat16),
            jax.ShapeDtypeStruct((2, 2 * rows_out, pairs, 2 * cin), jnp.bfloat16),
        ),
        cost_estimate=pl.CostEstimate(flops=100_000_000, bytes_accessed=1_000_000, transcendentals=0),
        compiler_params=pltpu.CompilerParams(vmem_limit_bytes=VMEM_BYTES),
        name="finish",
    )(rim, later, weight, forward, first, second)
    piece, output, grad_volume = lax.optimization_barrier((piece, output, grad_volume))
    copies = jnp.broadcast_to(piece.astype(jnp.bfloat16)[None], (count, rows, cout))
    gathered = exchange(copies, SLAB)
    grad_weight = pl.pallas_call(
        lambda chunks_ref, grad_ref: spread_kernel(step, factor, chunks_ref, grad_ref),
        out_shape=jax.ShapeDtypeStruct((total, cout), jnp.float32),
        compiler_params=pltpu.CompilerParams(vmem_limit_bytes=VMEM_BYTES),
        name="spread_out",
    )(gathered)
    return (output[None, None], grad_volume[None], grad_weight.reshape(weight.shape))


def solution(mesh):
    fine = jax.sharding.Mesh(mesh.devices.reshape(SIZES), DP + SPACE)
    split = P(DP, SPACE, None, None, None)
    return jax.shard_map(
        shards,
        mesh=fine,
        in_specs=(split, P(), split),
        out_specs=(split, split, P()),
        check_vma=False,
    )
```

```python
import math

import jax
import jax.numpy as jnp
from jax import lax
from jax.experimental import pallas as pl
from jax.experimental.pallas import tpu as pltpu
from jax.sharding import PartitionSpec as P

DP = ("x", "zh")
SPACE = ("y", "zn", "ze", "c")
SLAB = ("x", "y", "ze", "c")
LINE = ("zh", "zn")
SIZES = (4, 4, 4, 4, 2, 2)
VMEM_BYTES = 16 << 20


def passed_along(value, axes, steps):
    count = math.prod(lax.axis_size(axis) for axis in axes)
    first, last = (max(0, -steps), min(count, count - steps))
    return lax.ppermute(value, axes, [(source, source + steps) for source in range(first, last)])


def exchange(value, axes):
    return lax.all_to_all(value, axes, 0, 0, tiled=True)


def with_next_pair(cells, pairs):
    wide = cells.astype(jnp.float32)
    rows = wide.shape[0]
    row = lax.broadcasted_iota(jnp.int32, wide.shape, 0)
    ahead = jnp.where(row % pairs == pairs - 1, 0.0, pltpu.roll(wide, rows - 1, 0))
    return jnp.concatenate([cells, ahead.astype(jnp.bfloat16)], axis=1)


def from_previous_pair(wide, pairs):
    row = lax.broadcasted_iota(jnp.int32, wide.shape, 0)
    return jnp.where(row % pairs == 0, 0.0, pltpu.roll(wide, 1, 0))


def plane_rows(plane, rows_out):
    even = jnp.concatenate([plane[2 * b] for b in range(rows_out)], axis=0)
    odd = jnp.concatenate([plane[2 * b + 1] for b in range(rows_out)], axis=0)
    return even, odd


def tap_weight(weight, depth_tap, height_tap):
    taps = weight[depth_tap, height_tap]
    pair = jnp.concatenate([taps[1], taps[2]], axis=0)
    left = jnp.concatenate([jnp.zeros_like(taps[0]), taps[0]], axis=0)
    return jnp.concatenate([pair, left], axis=1)


def forward_dot(rows, weight):
    return lax.dot_general(
        rows, weight, (((1,), (0,)), ((), ())), preferred_element_type=jnp.float32
    )


def backward_dot(rows, weight):
    return lax.dot_general(
        rows, weight, (((1,), (1,)), ((), ())), preferred_element_type=jnp.float32
    )


def kernel_dot(rows, grads):
    return lax.dot_general(
        rows, grads, (((0,), (0,)), ((), ())), preferred_element_type=jnp.float32
    )


def store_kernel_terms(terms_ref, depth_tap, plane, grads, rows_out, pairs, cin, cout):
    even, odd = plane_rows(plane, rows_out)
    kept = (rows_out - 1) * pairs
    products = (
        kernel_dot(odd[:kept], grads[pairs:]),
        kernel_dot(even, grads),
        kernel_dot(odd, grads),
    )
    for height_tap in range(3):
        product = products[height_tap]
        base = (depth_tap * 3 + height_tap) * 3 * cin
        terms_ref[base : base + cin] = product[cin:, cout:]
        terms_ref[base + cin : base + 3 * cin] = product[:, :cout]


def forward_terms(plane, weight, depth_tap, rows_out, pairs):
    even, odd = plane_rows(plane, rows_out)
    lifted = jnp.concatenate([jnp.zeros_like(odd[:pairs]), odd[: (rows_out - 1) * pairs]], axis=0)
    return (
        forward_dot(lifted, tap_weight(weight, depth_tap, 0))
        + forward_dot(even, tap_weight(weight, depth_tap, 1))
        + forward_dot(odd, tap_weight(weight, depth_tap, 2))
    )


def backward_terms(grads, weight, depth_tap, pairs):
    raised = jnp.concatenate([grads[pairs:], jnp.zeros_like(grads[:pairs])], axis=0)
    even = backward_dot(grads, tap_weight(weight, depth_tap, 1))
    odd = backward_dot(grads, tap_weight(weight, depth_tap, 2)) + backward_dot(
        raised, tap_weight(weight, depth_tap, 0)
    )
    return even, odd


def own_kernel(local_ref, grads_ref, weight_ref, terms_ref, forward_ref, first_ref, second_ref):
    rows_out, pairs, cout = grads_ref.shape
    cin = weight_ref.shape[3]
    grads = with_next_pair(grads_ref[...].reshape(rows_out * pairs, cout), pairs)
    for depth_tap in (1, 2):
        plane = local_ref[depth_tap - 1]
        store_kernel_terms(terms_ref, depth_tap - 1, plane, grads, rows_out, pairs, cin, cout)
    forward_ref[...] = forward_terms(local_ref[0], weight_ref, 1, rows_out, pairs) + forward_terms(
        local_ref[1], weight_ref, 2, rows_out, pairs
    )
    even, odd = backward_terms(grads, weight_ref, 1, pairs)
    for b in range(rows_out):
        first_ref[2 * b] = even[b * pairs : (b + 1) * pairs].astype(jnp.bfloat16)
        first_ref[2 * b + 1] = odd[b * pairs : (b + 1) * pairs].astype(jnp.bfloat16)
    even, odd = backward_terms(grads, weight_ref, 2, pairs)
    second_ref[0] = even
    second_ref[1] = odd


def joined_kernel(local_ref, later_ref, terms_ref, chunks_ref, scratch_ref):
    rows_out, pairs, cout = later_ref.shape
    cin = local_ref.shape[3] // 2
    count, rows, _ = chunks_ref.shape
    total = 27 * cin
    step = total // count
    later = with_next_pair(later_ref[...].reshape(rows_out * pairs, cout), pairs)
    store_kernel_terms(scratch_ref, 0, local_ref[1], later, rows_out, pairs, cin, cout)
    scratch_ref[9 * cin : total] = terms_ref[...]
    scratch_ref[total:] = jnp.zeros((scratch_ref.shape[0] - total, cout), jnp.float32)
    for index in range(count):
        chunks_ref[index] = scratch_ref[index * step : index * step + rows].astype(chunks_ref.dtype)


def finish_kernel(
    rim_ref, later_ref, weight_ref, forward_ref, first_ref, second_ref, output_ref, grad_ref
):
    rows_out, pairs, cout = later_ref.shape
    later = with_next_pair(later_ref[...].reshape(rows_out * pairs, cout), pairs)
    total = forward_ref[...] + forward_terms(rim_ref[0], weight_ref, 0, rows_out, pairs)
    result = total[:, :cout] + from_previous_pair(total[:, cout:], pairs)
    output_ref[...] = result.astype(jnp.bfloat16).reshape(output_ref.shape)
    even, odd = backward_terms(later, weight_ref, 0, pairs)
    even = (even + second_ref[0]).astype(jnp.bfloat16)
    odd = (odd + second_ref[1]).astype(jnp.bfloat16)
    grad_ref[0] = first_ref[...]
    for b in range(rows_out):
        grad_ref[1, 2 * b] = even[b * pairs : (b + 1) * pairs]
        grad_ref[1, 2 * b + 1] = odd[b * pairs : (b + 1) * pairs]


def spread_kernel(step, factor, chunks_ref, grad_ref):
    for index in range(chunks_ref.shape[0]):
        block = chunks_ref[index].astype(jnp.float32)[:step]
        grad_ref[index * step : (index + 1) * step] = block * factor


def shards(volume, weight, cotangent):
    local = volume[0]
    grads = cotangent[0, 0]
    rows_out, pairs, cout = grads.shape
    cin = weight.shape[3]
    total = 27 * cin
    cells = rows_out * pairs
    count = math.prod(lax.axis_size(axis) for axis in SLAB)
    step = total // count
    rows = -(-step // 8) * 8
    devices = math.prod(lax.axis_size(axis) for axis in DP + SPACE)
    factor = 1.0 / math.sqrt(devices * cells)

    later = passed_along(grads, SPACE, -1)
    rim = passed_along(local[1:2], SPACE, 1)
    terms, forward, first, second = pl.pallas_call(
        own_kernel,
        out_shape=(
            jax.ShapeDtypeStruct((18 * cin, cout), jnp.float32),
            jax.ShapeDtypeStruct((cells, 2 * cout), jnp.float32),
            jax.ShapeDtypeStruct((2 * rows_out, pairs, 2 * cin), jnp.bfloat16),
            jax.ShapeDtypeStruct((2, cells, 2 * cin), jnp.float32),
        ),
        cost_estimate=pl.CostEstimate(flops=300_000_000, bytes_accessed=2_000_000, transcendentals=0),
        compiler_params=pltpu.CompilerParams(vmem_limit_bytes=VMEM_BYTES),
        name="own",
    )(local, grads, weight)
    chunks = pl.pallas_call(
        joined_kernel,
        out_shape=jax.ShapeDtypeStruct((count, rows, cout), jnp.bfloat16),
        scratch_shapes=[pltpu.VMEM((total + 8, cout), jnp.float32)],
        cost_estimate=pl.CostEstimate(flops=60_000_000, bytes_accessed=1_000_000, transcendentals=0),
        compiler_params=pltpu.CompilerParams(vmem_limit_bytes=VMEM_BYTES),
        name="joined",
    )(local, later, terms)

    piece = jnp.sum(exchange(chunks, SLAB).astype(jnp.float32), axis=0)
    piece, rim = lax.optimization_barrier((piece, rim))
    lines = math.prod(lax.axis_size(axis) for axis in LINE)
    copies = jnp.broadcast_to(piece.astype(jnp.bfloat16)[None], (lines, rows, cout))
    piece = jnp.sum(exchange(copies, LINE).astype(jnp.float32), axis=0)

    output, grad_volume = pl.pallas_call(
        finish_kernel,
        out_shape=(
            jax.ShapeDtypeStruct((rows_out, pairs, cout), jnp.bfloat16),
            jax.ShapeDtypeStruct((2, 2 * rows_out, pairs, 2 * cin), jnp.bfloat16),
        ),
        cost_estimate=pl.CostEstimate(flops=100_000_000, bytes_accessed=1_000_000, transcendentals=0),
        compiler_params=pltpu.CompilerParams(vmem_limit_bytes=VMEM_BYTES),
        name="finish",
    )(rim, later, weight, forward, first, second)
    piece, output, grad_volume = lax.optimization_barrier((piece, output, grad_volume))
    copies = jnp.broadcast_to(piece.astype(jnp.bfloat16)[None], (count, rows, cout))
    gathered = exchange(copies, SLAB)
    grad_weight = pl.pallas_call(
        lambda chunks_ref, grad_ref: spread_kernel(step, factor, chunks_ref, grad_ref),
        out_shape=jax.ShapeDtypeStruct((total, cout), jnp.float32),
        compiler_params=pltpu.CompilerParams(vmem_limit_bytes=VMEM_BYTES),
        name="spread_out",
    )(gathered)
    return (output[None, None], grad_volume[None], grad_weight.reshape(weight.shape))


def solution(mesh):
    fine = jax.sharding.Mesh(mesh.devices.reshape(SIZES), DP + SPACE)
    split = P(DP, SPACE, None, None, None)
    return jax.shard_map(
        shards,
        mesh=fine,
        in_specs=(split, P(), split),
        out_specs=(split, split, P()),
        check_vma=False,
    )
```

```python
import functools
import math

import jax
import jax.numpy as jnp
from jax import lax
from jax.experimental import pallas as pl
from jax.experimental.pallas import tpu as pltpu
from jax.sharding import PartitionSpec as P

DP = ("x", "zh")
SPACE = ("y", "zn", "ze", "c")
SLAB = ("x", "y", "ze", "c")
LINE = ("zh", "zn")
SIZES = (4, 4, 4, 4, 2, 2)
VMEM_BYTES = 16 << 20


def passed_along(value, axes, steps):
    count = math.prod(lax.axis_size(axis) for axis in axes)
    first, last = (max(0, -steps), min(count, count - steps))
    return lax.ppermute(value, axes, [(source, source + steps) for source in range(first, last)])


def exchange(value, axes):
    return lax.all_to_all(value, axes, 0, 0, tiled=True)


def with_next_pair(cells, pairs):
    wide = cells.astype(jnp.float32)
    rows = wide.shape[0]
    row = lax.broadcasted_iota(jnp.int32, wide.shape, 0)
    ahead = jnp.where(row % pairs == pairs - 1, 0.0, pltpu.roll(wide, rows - 1, 0))
    return jnp.concatenate([cells, ahead.astype(jnp.bfloat16)], axis=1)


def from_previous_pair(wide, pairs):
    row = lax.broadcasted_iota(jnp.int32, wide.shape, 0)
    return jnp.where(row % pairs == 0, 0.0, pltpu.roll(wide, 1, 0))


def plane_rows(plane, rows_out):
    even = jnp.concatenate([plane[2 * b] for b in range(rows_out)], axis=0)
    odd = jnp.concatenate([plane[2 * b + 1] for b in range(rows_out)], axis=0)
    return even, odd


def tap_weight(weight, depth_tap, height_tap):
    taps = weight[depth_tap, height_tap]
    pair = jnp.concatenate([taps[1], taps[2]], axis=0)
    left = jnp.concatenate([jnp.zeros_like(taps[0]), taps[0]], axis=0)
    return jnp.concatenate([pair, left], axis=1)


def forward_dot(rows, weight):
    return lax.dot_general(
        rows, weight, (((1,), (0,)), ((), ())), preferred_element_type=jnp.float32
    )


def backward_dot(rows, weight):
    return lax.dot_general(
        rows, weight, (((1,), (1,)), ((), ())), preferred_element_type=jnp.float32
    )


def kernel_dot(rows, grads):
    return lax.dot_general(
        rows, grads, (((0,), (0,)), ((), ())), preferred_element_type=jnp.float32
    )


def store_kernel_terms(terms_ref, base, plane, grads, rows_out, pairs, cin, cout):
    even, odd = plane_rows(plane, rows_out)
    kept = (rows_out - 1) * pairs
    products = (
        kernel_dot(odd[:kept], grads[pairs:]),
        kernel_dot(even, grads),
        kernel_dot(odd, grads),
    )
    for height_tap in range(3):
        product = products[height_tap]
        start = base + height_tap * 3 * cin
        terms_ref[start : start + cin] = product[cin:, cout:].astype(terms_ref.dtype)
        terms_ref[start + cin : start + 3 * cin] = product[:, :cout].astype(terms_ref.dtype)


def forward_terms(plane, weight, depth_tap, rows_out, pairs):
    even, odd = plane_rows(plane, rows_out)
    lifted = jnp.concatenate([jnp.zeros_like(odd[:pairs]), odd[: (rows_out - 1) * pairs]], axis=0)
    return (
        forward_dot(lifted, tap_weight(weight, depth_tap, 0))
        + forward_dot(even, tap_weight(weight, depth_tap, 1))
        + forward_dot(odd, tap_weight(weight, depth_tap, 2))
    )


def backward_terms(grads, weight, depth_tap, pairs):
    raised = jnp.concatenate([grads[pairs:], jnp.zeros_like(grads[:pairs])], axis=0)
    even = backward_dot(grads, tap_weight(weight, depth_tap, 1))
    odd = backward_dot(grads, tap_weight(weight, depth_tap, 2)) + backward_dot(
        raised, tap_weight(weight, depth_tap, 0)
    )
    return even, odd


def own_kernel(local_ref, grads_ref, head_ref, rest_ref, terms_ref):
    rows_out, pairs, cout = grads_ref.shape
    cin = local_ref.shape[3] // 2
    grads = with_next_pair(grads_ref[...].reshape(rows_out * pairs, cout), pairs)
    for plane in range(2):
        store_kernel_terms(
            terms_ref, plane * 9 * cin, local_ref[plane], grads, rows_out, pairs, cin, cout
        )
    kept = head_ref.shape[0]
    head_ref[...] = terms_ref[:kept]
    rest_ref[...] = terms_ref[kept:]


def joined_kernel(step, local_ref, later_ref, rest_ref, chunks_ref, scratch_ref):
    rows_out, pairs, cout = later_ref.shape
    cin = local_ref.shape[3] // 2
    count, rows, _ = chunks_ref.shape
    rest = rest_ref.shape[0]
    total = rest + 9 * cin
    later = with_next_pair(later_ref[...].reshape(rows_out * pairs, cout), pairs)
    scratch_ref[:rest] = rest_ref[...].astype(jnp.float32)
    store_kernel_terms(scratch_ref, rest, local_ref[1], later, rows_out, pairs, cin, cout)
    scratch_ref[total:] = jnp.zeros((scratch_ref.shape[0] - total, cout), jnp.float32)
    for index in range(count):
        chunks_ref[index] = scratch_ref[index * step : index * step + rows].astype(jnp.bfloat16)


def copies_kernel(first_ref, second_ref, copies_ref):
    first = jnp.sum(first_ref[...].astype(jnp.float32), axis=0).astype(jnp.bfloat16)
    second = jnp.sum(second_ref[...].astype(jnp.float32), axis=0).astype(jnp.bfloat16)
    piece = jnp.concatenate([first, second], axis=0)
    for index in range(copies_ref.shape[0]):
        copies_ref[index] = piece


def finish_kernel(
    rim_ref, local_ref, grads_ref, later_ref, weight_ref, output_ref, grad_ref
):
    rows_out, pairs, cout = later_ref.shape
    cells = rows_out * pairs
    grads = with_next_pair(grads_ref[...].reshape(cells, cout), pairs)
    later = with_next_pair(later_ref[...].reshape(cells, cout), pairs)
    total = (
        forward_terms(rim_ref[0], weight_ref, 0, rows_out, pairs)
        + forward_terms(local_ref[0], weight_ref, 1, rows_out, pairs)
        + forward_terms(local_ref[1], weight_ref, 2, rows_out, pairs)
    )
    result = total[:, :cout] + from_previous_pair(total[:, cout:], pairs)
    output_ref[...] = result.astype(jnp.bfloat16).reshape(output_ref.shape)
    spilled = backward_terms(later, weight_ref, 0, pairs)
    own = backward_terms(grads, weight_ref, 2, pairs)
    planes = (
        backward_terms(grads, weight_ref, 1, pairs),
        (spilled[0] + own[0], spilled[1] + own[1]),
    )
    for plane, sides in enumerate(planes):
        for side, values in enumerate(sides):
            rounded = values.astype(jnp.bfloat16)
            for b in range(rows_out):
                grad_ref[plane, 2 * b + side] = rounded[b * pairs : (b + 1) * pairs]


def spread_kernel(head, step, cin, factor, chunks_ref, grad_ref):
    count = chunks_ref.shape[0]
    ahead = 9 * cin
    total = 27 * cin
    for index in range(count):
        block = chunks_ref[index].astype(jnp.float32) * factor
        grad_ref[ahead + index * head : ahead + (index + 1) * head] = block[:head]
        start = ahead + count * head + index * step
        stop = start + step
        below = min(max(total - start, 0), step)
        if below:
            grad_ref[start : start + below] = block[head : head + below]
        if below < step:
            grad_ref[start + below - total : stop - total] = block[head + below : head + step]


def shards(volume, weight, cotangent):
    local = volume[0]
    grads = cotangent[0, 0]
    rows_out, pairs, cout = grads.shape
    cin = weight.shape[3]
    total = 27 * cin
    cells = rows_out * pairs
    count = math.prod(lax.axis_size(axis) for axis in SLAB)
    head = 18 * cin // count // 16 * 16
    step = total // count - head
    rows = -(-step // 16) * 16
    devices = math.prod(lax.axis_size(axis) for axis in DP + SPACE)
    factor = 1.0 / math.sqrt(devices * cells)

    later = passed_along(grads, SPACE, -1)
    rim = passed_along(local[1:2], SPACE, 1)
    kept = count * head
    leaving, rest = pl.pallas_call(
        own_kernel,
        out_shape=(
            jax.ShapeDtypeStruct((kept, cout), jnp.bfloat16),
            jax.ShapeDtypeStruct((18 * cin - kept, cout), jnp.bfloat16),
        ),
        scratch_shapes=[pltpu.VMEM((18 * cin, cout), jnp.bfloat16)],
        cost_estimate=pl.CostEstimate(flops=100_000_000, bytes_accessed=600_000, transcendentals=0),
        compiler_params=pltpu.CompilerParams(vmem_limit_bytes=VMEM_BYTES),
        name="own",
    )(local, grads)
    first = exchange(leaving.reshape(count, head, cout), SLAB)
    chunks = pl.pallas_call(
        functools.partial(joined_kernel, step),
        out_shape=jax.ShapeDtypeStruct((count, rows, cout), jnp.bfloat16),
        scratch_shapes=[pltpu.VMEM((count * step + 16, cout), jnp.float32)],
        cost_estimate=pl.CostEstimate(flops=40_000_000_000, bytes_accessed=600_000, transcendentals=0),
        compiler_params=pltpu.CompilerParams(vmem_limit_bytes=VMEM_BYTES),
        name="joined",
    )(local, later, rest)
    second = exchange(chunks, SLAB)
    first, second, rim = lax.optimization_barrier((first, second, rim))
    lines = math.prod(lax.axis_size(axis) for axis in LINE)
    copies = pl.pallas_call(
        copies_kernel,
        out_shape=jax.ShapeDtypeStruct((lines, head + rows, cout), jnp.bfloat16),
        cost_estimate=pl.CostEstimate(flops=500_000, bytes_accessed=700_000, transcendentals=0),
        compiler_params=pltpu.CompilerParams(vmem_limit_bytes=VMEM_BYTES),
        name="copies",
    )(first, second)
    piece = jnp.sum(exchange(copies, LINE).astype(jnp.float32), axis=0)

    output, grad_volume = pl.pallas_call(
        finish_kernel,
        out_shape=(
            jax.ShapeDtypeStruct((rows_out, pairs, cout), jnp.bfloat16),
            jax.ShapeDtypeStruct((2, 2 * rows_out, pairs, 2 * cin), jnp.bfloat16),
        ),
        cost_estimate=pl.CostEstimate(flops=400_000_000, bytes_accessed=1_500_000, transcendentals=0),
        compiler_params=pltpu.CompilerParams(vmem_limit_bytes=VMEM_BYTES),
        name="finish",
    )(rim, local, grads, later, weight)
    piece, output, grad_volume = lax.optimization_barrier((piece, output, grad_volume))
    copies = jnp.broadcast_to(piece.astype(jnp.bfloat16)[None], (count, head + rows, cout))
    gathered = exchange(copies, SLAB)
    grad_weight = pl.pallas_call(
        functools.partial(spread_kernel, head, step, cin, factor),
        out_shape=jax.ShapeDtypeStruct((total, cout), jnp.float32),
        compiler_params=pltpu.CompilerParams(vmem_limit_bytes=VMEM_BYTES),
        name="spread_out",
    )(gathered)
    return (output[None, None], grad_volume[None], grad_weight.reshape(weight.shape))


def solution(mesh):
    fine = jax.sharding.Mesh(mesh.devices.reshape(SIZES), DP + SPACE)
    split = P(DP, SPACE, None, None, None)
    return jax.shard_map(
        shards,
        mesh=fine,
        in_specs=(split, P(), split),
        out_specs=(split, split, P()),
        check_vma=False,
    )
```

```python
import functools
import math

import jax
import jax.numpy as jnp
from jax import lax
from jax.experimental import pallas as pl
from jax.experimental.pallas import tpu as pltpu
from jax.sharding import PartitionSpec as P

DP = ("x", "zh")
SPACE = ("y", "zn", "ze", "c")
SLAB = ("x", "y", "ze", "c")
LINE = ("zh", "zn")
SIZES = (4, 4, 4, 4, 2, 2)
VMEM_BYTES = 16 << 20


def passed_along(value, axes, steps):
    count = math.prod(lax.axis_size(axis) for axis in axes)
    first, last = (max(0, -steps), min(count, count - steps))
    return lax.ppermute(value, axes, [(source, source + steps) for source in range(first, last)])


def exchange(value, axes):
    return lax.all_to_all(value, axes, 0, 0, tiled=True)


def with_next_pair(cells, pairs):
    wide = cells.astype(jnp.float32)
    rows = wide.shape[0]
    row = lax.broadcasted_iota(jnp.int32, wide.shape, 0)
    ahead = jnp.where(row % pairs == pairs - 1, 0.0, pltpu.roll(wide, rows - 1, 0))
    return jnp.concatenate([cells, ahead.astype(jnp.bfloat16)], axis=1)


def from_previous_pair(wide, pairs):
    row = lax.broadcasted_iota(jnp.int32, wide.shape, 0)
    return jnp.where(row % pairs == 0, 0.0, pltpu.roll(wide, 1, 0))


def plane_rows(plane, rows_out):
    even = jnp.concatenate([plane[2 * b] for b in range(rows_out)], axis=0)
    odd = jnp.concatenate([plane[2 * b + 1] for b in range(rows_out)], axis=0)
    return even, odd


def tap_weight(weight, depth_tap, height_tap):
    taps = weight[depth_tap, height_tap]
    pair = jnp.concatenate([taps[1], taps[2]], axis=0)
    left = jnp.concatenate([jnp.zeros_like(taps[0]), taps[0]], axis=0)
    return jnp.concatenate([pair, left], axis=1)


def forward_dot(rows, weight):
    return lax.dot_general(
        rows, weight, (((1,), (0,)), ((), ())), preferred_element_type=jnp.float32
    )


def backward_dot(rows, weight):
    return lax.dot_general(
        rows, weight, (((1,), (1,)), ((), ())), preferred_element_type=jnp.float32
    )


def kernel_dot(rows, grads):
    return lax.dot_general(
        rows, grads, (((0,), (0,)), ((), ())), preferred_element_type=jnp.float32
    )


def store_kernel_terms(terms_ref, base, plane, grads, rows_out, pairs, cin, cout):
    even, odd = plane_rows(plane, rows_out)
    kept = (rows_out - 1) * pairs
    products = (
        kernel_dot(odd[:kept], grads[pairs:]),
        kernel_dot(even, grads),
        kernel_dot(odd, grads),
    )
    for height_tap in range(3):
        product = products[height_tap]
        start = base + height_tap * 3 * cin
        terms_ref[start : start + cin] = product[cin:, cout:].astype(terms_ref.dtype)
        terms_ref[start + cin : start + 3 * cin] = product[:, :cout].astype(terms_ref.dtype)


def forward_terms(plane, weight, depth_tap, rows_out, pairs):
    even, odd = plane_rows(plane, rows_out)
    lifted = jnp.concatenate([jnp.zeros_like(odd[:pairs]), odd[: (rows_out - 1) * pairs]], axis=0)
    return (
        forward_dot(lifted, tap_weight(weight, depth_tap, 0))
        + forward_dot(even, tap_weight(weight, depth_tap, 1))
        + forward_dot(odd, tap_weight(weight, depth_tap, 2))
    )


def backward_terms(grads, weight, depth_tap, pairs):
    raised = jnp.concatenate([grads[pairs:], jnp.zeros_like(grads[:pairs])], axis=0)
    even = backward_dot(grads, tap_weight(weight, depth_tap, 1))
    odd = backward_dot(grads, tap_weight(weight, depth_tap, 2)) + backward_dot(
        raised, tap_weight(weight, depth_tap, 0)
    )
    return even, odd


def own_kernel(local_ref, grads_ref, terms_ref, plane_ref):
    rows_out, pairs, cout = grads_ref.shape
    cin = local_ref.shape[3] // 2
    grads = with_next_pair(grads_ref[...].reshape(rows_out * pairs, cout), pairs)
    for plane in range(2):
        store_kernel_terms(
            terms_ref, plane * 9 * cin, local_ref[plane], grads, rows_out, pairs, cin, cout
        )
    plane_ref[0] = local_ref[1]


def joined_kernel(local_ref, later_ref, terms_ref, chunks_ref, scratch_ref):
    rows_out, pairs, cout = later_ref.shape
    cin = local_ref.shape[3] // 2
    count, rows, _ = chunks_ref.shape
    total = 27 * cin
    step = total // count
    later = with_next_pair(later_ref[...].reshape(rows_out * pairs, cout), pairs)
    store_kernel_terms(scratch_ref, 0, local_ref[1], later, rows_out, pairs, cin, cout)
    scratch_ref[9 * cin : total] = terms_ref[...]
    scratch_ref[total:] = jnp.zeros((scratch_ref.shape[0] - total, cout), jnp.float32)
    for index in range(count):
        chunks_ref[index] = scratch_ref[index * step : index * step + rows].astype(jnp.bfloat16)


def copies_kernel(chunks_ref, copies_ref):
    piece = jnp.sum(chunks_ref[...].astype(jnp.float32), axis=0).astype(jnp.bfloat16)
    for index in range(copies_ref.shape[0]):
        copies_ref[index] = piece


def finish_kernel(
    rim_ref, local_ref, grads_ref, later_ref, weight_ref, output_ref, grad_ref
):
    rows_out, pairs, cout = later_ref.shape
    cells = rows_out * pairs
    grads = with_next_pair(grads_ref[...].reshape(cells, cout), pairs)
    later = with_next_pair(later_ref[...].reshape(cells, cout), pairs)
    total = (
        forward_terms(rim_ref[0], weight_ref, 0, rows_out, pairs)
        + forward_terms(local_ref[0], weight_ref, 1, rows_out, pairs)
        + forward_terms(local_ref[1], weight_ref, 2, rows_out, pairs)
    )
    result = total[:, :cout] + from_previous_pair(total[:, cout:], pairs)
    output_ref[...] = result.astype(jnp.bfloat16).reshape(output_ref.shape)
    spilled = backward_terms(later, weight_ref, 0, pairs)
    own = backward_terms(grads, weight_ref, 2, pairs)
    planes = (
        backward_terms(grads, weight_ref, 1, pairs),
        (spilled[0] + own[0], spilled[1] + own[1]),
    )
    for plane, sides in enumerate(planes):
        for side, values in enumerate(sides):
            rounded = values.astype(jnp.bfloat16)
            for b in range(rows_out):
                grad_ref[plane, 2 * b + side] = rounded[b * pairs : (b + 1) * pairs]


def spread_kernel(step, factor, chunks_ref, grad_ref):
    for index in range(chunks_ref.shape[0]):
        block = chunks_ref[index].astype(jnp.float32)[:step]
        grad_ref[index * step : (index + 1) * step] = block * factor


def shards(volume, weight, cotangent):
    local = volume[0]
    grads = cotangent[0, 0]
    rows_out, pairs, cout = grads.shape
    cin = weight.shape[3]
    total = 27 * cin
    cells = rows_out * pairs
    count = math.prod(lax.axis_size(axis) for axis in SLAB)
    step = total // count
    rows = -(-step // 16) * 16
    devices = math.prod(lax.axis_size(axis) for axis in DP + SPACE)
    factor = 1.0 / math.sqrt(devices * cells)

    later = passed_along(grads, SPACE, -1)
    terms, plane = pl.pallas_call(
        own_kernel,
        out_shape=(
            jax.ShapeDtypeStruct((18 * cin, cout), jnp.float32),
            jax.ShapeDtypeStruct((1, *local.shape[1:]), jnp.bfloat16),
        ),
        cost_estimate=pl.CostEstimate(flops=300_000_000, bytes_accessed=2_000_000, transcendentals=0),
        compiler_params=pltpu.CompilerParams(vmem_limit_bytes=VMEM_BYTES),
        name="own",
    )(local, grads)
    chunks = pl.pallas_call(
        joined_kernel,
        out_shape=jax.ShapeDtypeStruct((count, rows, cout), jnp.bfloat16),
        scratch_shapes=[pltpu.VMEM((total + 16, cout), jnp.float32)],
        cost_estimate=pl.CostEstimate(flops=60_000_000, bytes_accessed=1_000_000, transcendentals=0),
        compiler_params=pltpu.CompilerParams(vmem_limit_bytes=VMEM_BYTES),
        name="joined",
    )(local, later, terms)
    lines = math.prod(lax.axis_size(axis) for axis in LINE)
    copies = pl.pallas_call(
        copies_kernel,
        out_shape=jax.ShapeDtypeStruct((lines, rows, cout), jnp.bfloat16),
        cost_estimate=pl.CostEstimate(flops=500_000, bytes_accessed=700_000, transcendentals=0),
        compiler_params=pltpu.CompilerParams(vmem_limit_bytes=VMEM_BYTES),
        name="copies",
    )(exchange(chunks, SLAB))
    copies, plane, later, local, grads = lax.optimization_barrier(
        (copies, plane, later, local, grads)
    )
    rim = passed_along(plane, SPACE, 1)
    piece = jnp.sum(exchange(copies, LINE).astype(jnp.float32), axis=0)

    output, grad_volume = pl.pallas_call(
        finish_kernel,
        out_shape=(
            jax.ShapeDtypeStruct((rows_out, pairs, cout), jnp.bfloat16),
            jax.ShapeDtypeStruct((2, 2 * rows_out, pairs, 2 * cin), jnp.bfloat16),
        ),
        cost_estimate=pl.CostEstimate(flops=400_000_000, bytes_accessed=1_500_000, transcendentals=0),
        compiler_params=pltpu.CompilerParams(vmem_limit_bytes=VMEM_BYTES),
        name="finish",
    )(rim, local, grads, later, weight)
    piece, output, grad_volume = lax.optimization_barrier((piece, output, grad_volume))
    copies = jnp.broadcast_to(piece.astype(jnp.bfloat16)[None], (count, rows, cout))
    gathered = exchange(copies, SLAB)
    grad_weight = pl.pallas_call(
        functools.partial(spread_kernel, step, factor),
        out_shape=jax.ShapeDtypeStruct((total, cout), jnp.float32),
        compiler_params=pltpu.CompilerParams(vmem_limit_bytes=VMEM_BYTES),
        name="spread_out",
    )(gathered)
    return (output[None, None], grad_volume[None], grad_weight.reshape(weight.shape))


def solution(mesh):
    fine = jax.sharding.Mesh(mesh.devices.reshape(SIZES), DP + SPACE)
    split = P(DP, SPACE, None, None, None)
    return jax.shard_map(
        shards,
        mesh=fine,
        in_specs=(split, P(), split),
        out_specs=(split, split, P()),
        check_vma=False,
    )
```

```python
import functools
import math

import jax
import jax.numpy as jnp
from jax import lax
from jax.experimental import pallas as pl
from jax.experimental.pallas import tpu as pltpu
from jax.sharding import PartitionSpec as P

DP = ("x", "zh")
SPACE = ("y", "zn", "ze", "c")
SLAB = ("x", "y", "ze")
LINE = ("zh", "zn")
SIZES = (4, 4, 4, 4, 2, 2)
VMEM_BYTES = 16 << 20


def passed_along(value, axes, steps):
    count = math.prod(lax.axis_size(axis) for axis in axes)
    first, last = (max(0, -steps), min(count, count - steps))
    return lax.ppermute(value, axes, [(source, source + steps) for source in range(first, last)])


def exchange(value, axes):
    return lax.all_to_all(value, axes, 0, 0, tiled=True)


def with_next_pair(cells, pairs):
    wide = cells.astype(jnp.float32)
    rows = wide.shape[0]
    row = lax.broadcasted_iota(jnp.int32, wide.shape, 0)
    ahead = jnp.where(row % pairs == pairs - 1, 0.0, pltpu.roll(wide, rows - 1, 0))
    return jnp.concatenate([cells, ahead.astype(jnp.bfloat16)], axis=1)


def from_previous_pair(wide, pairs):
    row = lax.broadcasted_iota(jnp.int32, wide.shape, 0)
    return jnp.where(row % pairs == 0, 0.0, pltpu.roll(wide, 1, 0))


def plane_rows(plane, rows_out):
    even = jnp.concatenate([plane[2 * b] for b in range(rows_out)], axis=0)
    odd = jnp.concatenate([plane[2 * b + 1] for b in range(rows_out)], axis=0)
    return even, odd


def tap_weight(weight, depth_tap, height_tap):
    taps = weight[depth_tap, height_tap]
    pair = jnp.concatenate([taps[1], taps[2]], axis=0)
    left = jnp.concatenate([jnp.zeros_like(taps[0]), taps[0]], axis=0)
    return jnp.concatenate([pair, left], axis=1)


def forward_dot(rows, weight):
    return lax.dot_general(
        rows, weight, (((1,), (0,)), ((), ())), preferred_element_type=jnp.float32
    )


def backward_dot(rows, weight):
    return lax.dot_general(
        rows, weight, (((1,), (1,)), ((), ())), preferred_element_type=jnp.float32
    )


def kernel_dot(rows, grads):
    return lax.dot_general(
        rows, grads, (((0,), (0,)), ((), ())), preferred_element_type=jnp.float32
    )


def store_kernel_terms(terms_ref, base, plane, grads, rows_out, pairs, cin, cout):
    even, odd = plane_rows(plane, rows_out)
    kept = (rows_out - 1) * pairs
    products = (
        kernel_dot(odd[:kept], grads[pairs:]),
        kernel_dot(even, grads),
        kernel_dot(odd, grads),
    )
    for height_tap in range(3):
        product = products[height_tap]
        start = base + height_tap * 3 * cin
        terms_ref[start : start + cin] = product[cin:, cout:].astype(terms_ref.dtype)
        terms_ref[start + cin : start + 3 * cin] = product[:, :cout].astype(terms_ref.dtype)


def forward_terms(plane, weight, depth_tap, rows_out, pairs):
    even, odd = plane_rows(plane, rows_out)
    lifted = jnp.concatenate([jnp.zeros_like(odd[:pairs]), odd[: (rows_out - 1) * pairs]], axis=0)
    return (
        forward_dot(lifted, tap_weight(weight, depth_tap, 0))
        + forward_dot(even, tap_weight(weight, depth_tap, 1))
        + forward_dot(odd, tap_weight(weight, depth_tap, 2))
    )


def backward_terms(grads, weight, depth_tap, pairs):
    raised = jnp.concatenate([grads[pairs:], jnp.zeros_like(grads[:pairs])], axis=0)
    even = backward_dot(grads, tap_weight(weight, depth_tap, 1))
    odd = backward_dot(grads, tap_weight(weight, depth_tap, 2)) + backward_dot(
        raised, tap_weight(weight, depth_tap, 0)
    )
    return even, odd


def own_kernel(local_ref, grads_ref, terms_ref, plane_ref):
    rows_out, pairs, cout = grads_ref.shape
    cin = local_ref.shape[3] // 2
    grads = with_next_pair(grads_ref[...].reshape(rows_out * pairs, cout), pairs)
    for plane in range(2):
        store_kernel_terms(
            terms_ref, plane * 9 * cin, local_ref[plane], grads, rows_out, pairs, cin, cout
        )
    plane_ref[0] = local_ref[1]


def joined_kernel(core_ref, local_ref, later_ref, terms_ref, kept_ref, sent_ref, scratch_ref):
    rows_out, pairs, cout = later_ref.shape
    cin = local_ref.shape[3] // 2
    count, rows, _ = kept_ref.shape
    total = 27 * cin
    step = total // (2 * count)
    later = with_next_pair(later_ref[...].reshape(rows_out * pairs, cout), pairs)
    store_kernel_terms(scratch_ref, 0, local_ref[1], later, rows_out, pairs, cin, cout)
    scratch_ref[9 * cin : total] = terms_ref[...]
    scratch_ref[total:] = jnp.zeros((scratch_ref.shape[0] - total, cout), jnp.float32)
    first = core_ref[0] == 0
    for index in range(count):
        start = 2 * index * step
        even = scratch_ref[start : start + rows]
        odd = scratch_ref[start + step : start + step + rows]
        kept_ref[index] = jnp.where(first, even, odd)
        sent_ref[index] = jnp.where(first, odd, even)


def merge_kernel(kept_ref, other_ref, chunks_ref):
    chunks_ref[...] = (kept_ref[...] + other_ref[...]).astype(jnp.bfloat16)


def copies_kernel(chunks_ref, copies_ref):
    piece = jnp.sum(chunks_ref[...].astype(jnp.float32), axis=0).astype(jnp.bfloat16)
    for index in range(copies_ref.shape[0]):
        copies_ref[index] = piece


def finish_kernel(
    rim_ref, local_ref, grads_ref, later_ref, weight_ref, output_ref, grad_ref
):
    rows_out, pairs, cout = later_ref.shape
    cells = rows_out * pairs
    grads = with_next_pair(grads_ref[...].reshape(cells, cout), pairs)
    later = with_next_pair(later_ref[...].reshape(cells, cout), pairs)
    total = (
        forward_terms(rim_ref[0], weight_ref, 0, rows_out, pairs)
        + forward_terms(local_ref[0], weight_ref, 1, rows_out, pairs)
        + forward_terms(local_ref[1], weight_ref, 2, rows_out, pairs)
    )
    result = total[:, :cout] + from_previous_pair(total[:, cout:], pairs)
    output_ref[...] = result.astype(jnp.bfloat16).reshape(output_ref.shape)
    spilled = backward_terms(later, weight_ref, 0, pairs)
    own = backward_terms(grads, weight_ref, 2, pairs)
    planes = (
        backward_terms(grads, weight_ref, 1, pairs),
        (spilled[0] + own[0], spilled[1] + own[1]),
    )
    for plane, sides in enumerate(planes):
        for side, values in enumerate(sides):
            rounded = values.astype(jnp.bfloat16)
            for b in range(rows_out):
                grad_ref[plane, 2 * b + side] = rounded[b * pairs : (b + 1) * pairs]


def spread_kernel(step, factor, core_ref, own_ref, other_ref, grad_ref):
    first = core_ref[0] == 0
    for index in range(own_ref.shape[0]):
        own = own_ref[index].astype(jnp.float32)[:step] * factor
        other = other_ref[index].astype(jnp.float32)[:step] * factor
        start = 2 * index * step
        grad_ref[start : start + step] = jnp.where(first, own, other)
        grad_ref[start + step : start + 2 * step] = jnp.where(first, other, own)


def swapped(value):
    return lax.ppermute(value, "c", [(0, 1), (1, 0)])


def shards(volume, weight, cotangent):
    local = volume[0]
    grads = cotangent[0, 0]
    rows_out, pairs, cout = grads.shape
    cin = weight.shape[3]
    total = 27 * cin
    cells = rows_out * pairs
    count = math.prod(lax.axis_size(axis) for axis in SLAB)
    step = total // (2 * count)
    rows = -(-step // 16) * 16
    devices = math.prod(lax.axis_size(axis) for axis in DP + SPACE)
    factor = 1.0 / math.sqrt(devices * cells)

    later = passed_along(grads, SPACE, -1)
    terms, plane = pl.pallas_call(
        own_kernel,
        out_shape=(
            jax.ShapeDtypeStruct((18 * cin, cout), jnp.float32),
            jax.ShapeDtypeStruct((1, *local.shape[1:]), jnp.bfloat16),
        ),
        cost_estimate=pl.CostEstimate(flops=300_000_000, bytes_accessed=2_000_000, transcendentals=0),
        compiler_params=pltpu.CompilerParams(vmem_limit_bytes=VMEM_BYTES),
        name="own",
    )(local, grads)
    core = jnp.full((1,), lax.axis_index("c"), jnp.int32)
    in_vmem = pl.BlockSpec(memory_space=pltpu.VMEM)
    in_smem = pl.BlockSpec(memory_space=pltpu.SMEM)
    kept, sent = pl.pallas_call(
        joined_kernel,
        in_specs=[in_smem, in_vmem, in_vmem, in_vmem],
        out_shape=(
            jax.ShapeDtypeStruct((count, rows, cout), jnp.float32),
            jax.ShapeDtypeStruct((count, rows, cout), jnp.float32),
        ),
        scratch_shapes=[pltpu.VMEM((total + 16, cout), jnp.float32)],
        cost_estimate=pl.CostEstimate(flops=60_000_000, bytes_accessed=1_000_000, transcendentals=0),
        compiler_params=pltpu.CompilerParams(vmem_limit_bytes=VMEM_BYTES),
        name="joined",
    )(core, local, later, terms)
    chunks = pl.pallas_call(
        merge_kernel,
        out_shape=jax.ShapeDtypeStruct((count, rows, cout), jnp.bfloat16),
        cost_estimate=pl.CostEstimate(flops=500_000, bytes_accessed=1_000_000, transcendentals=0),
        compiler_params=pltpu.CompilerParams(vmem_limit_bytes=VMEM_BYTES),
        name="merge",
    )(kept, swapped(sent))
    lines = math.prod(lax.axis_size(axis) for axis in LINE)
    copies = pl.pallas_call(
        copies_kernel,
        out_shape=jax.ShapeDtypeStruct((lines, rows, cout), jnp.bfloat16),
        cost_estimate=pl.CostEstimate(flops=500_000, bytes_accessed=700_000, transcendentals=0),
        compiler_params=pltpu.CompilerParams(vmem_limit_bytes=VMEM_BYTES),
        name="copies",
    )(exchange(chunks, SLAB))
    copies, plane, later, local, grads = lax.optimization_barrier(
        (copies, plane, later, local, grads)
    )
    rim = passed_along(plane, SPACE, 1)
    piece = jnp.sum(exchange(copies, LINE).astype(jnp.float32), axis=0)

    output, grad_volume = pl.pallas_call(
        finish_kernel,
        out_shape=(
            jax.ShapeDtypeStruct((rows_out, pairs, cout), jnp.bfloat16),
            jax.ShapeDtypeStruct((2, 2 * rows_out, pairs, 2 * cin), jnp.bfloat16),
        ),
        cost_estimate=pl.CostEstimate(flops=400_000_000, bytes_accessed=1_500_000, transcendentals=0),
        compiler_params=pltpu.CompilerParams(vmem_limit_bytes=VMEM_BYTES),
        name="finish",
    )(rim, local, grads, later, weight)
    piece, output, grad_volume = lax.optimization_barrier((piece, output, grad_volume))
    copies = jnp.broadcast_to(piece.astype(jnp.bfloat16)[None], (count, rows, cout))
    gathered = exchange(copies, SLAB)
    grad_weight = pl.pallas_call(
        functools.partial(spread_kernel, step, factor),
        in_specs=[in_smem, in_vmem, in_vmem],
        out_shape=jax.ShapeDtypeStruct((total, cout), jnp.float32),
        compiler_params=pltpu.CompilerParams(vmem_limit_bytes=VMEM_BYTES),
        name="spread_out",
    )(core, gathered, swapped(gathered))
    return (output[None, None], grad_volume[None], grad_weight.reshape(weight.shape))


def solution(mesh):
    fine = jax.sharding.Mesh(mesh.devices.reshape(SIZES), DP + SPACE)
    split = P(DP, SPACE, None, None, None)
    return jax.shard_map(
        shards,
        mesh=fine,
        in_specs=(split, P(), split),
        out_specs=(split, split, P()),
        check_vma=False,
    )
```

```python
import functools
import math

import jax
import jax.numpy as jnp
from jax import lax
from jax.experimental import pallas as pl
from jax.experimental.pallas import tpu as pltpu
from jax.sharding import PartitionSpec as P

DP = ("x", "zh")
SPACE = ("y", "zp", "zq", "ze", "c")
SLAB = ("x", "y", "zq", "ze")
LINE = ("zh", "zp")
SIZES = (4, 4, 4, 2, 2, 2, 2)
VMEM_BYTES = 16 << 20


def passed_along(value, axes, steps):
    count = math.prod(lax.axis_size(axis) for axis in axes)
    first, last = (max(0, -steps), min(count, count - steps))
    return lax.ppermute(value, axes, [(source, source + steps) for source in range(first, last)])


def exchange(value, axes):
    return lax.all_to_all(value, axes, 0, 0, tiled=True)


def with_next_pair(cells, pairs):
    wide = cells.astype(jnp.float32)
    rows = wide.shape[0]
    row = lax.broadcasted_iota(jnp.int32, wide.shape, 0)
    ahead = jnp.where(row % pairs == pairs - 1, 0.0, pltpu.roll(wide, rows - 1, 0))
    return jnp.concatenate([cells, ahead.astype(jnp.bfloat16)], axis=1)


def from_previous_pair(wide, pairs):
    row = lax.broadcasted_iota(jnp.int32, wide.shape, 0)
    return jnp.where(row % pairs == 0, 0.0, pltpu.roll(wide, 1, 0))


def plane_rows(plane, rows_out):
    even = jnp.concatenate([plane[2 * b] for b in range(rows_out)], axis=0)
    odd = jnp.concatenate([plane[2 * b + 1] for b in range(rows_out)], axis=0)
    return even, odd


def tap_weight(weight, depth_tap, height_tap):
    taps = weight[depth_tap, height_tap]
    pair = jnp.concatenate([taps[1], taps[2]], axis=0)
    left = jnp.concatenate([jnp.zeros_like(taps[0]), taps[0]], axis=0)
    return jnp.concatenate([pair, left], axis=1)


def forward_dot(rows, weight):
    return lax.dot_general(
        rows, weight, (((1,), (0,)), ((), ())), preferred_element_type=jnp.float32
    )


def backward_dot(rows, weight):
    return lax.dot_general(
        rows, weight, (((1,), (1,)), ((), ())), preferred_element_type=jnp.float32
    )


def kernel_dot(rows, grads):
    return lax.dot_general(
        rows, grads, (((0,), (0,)), ((), ())), preferred_element_type=jnp.float32
    )


def store_kernel_terms(terms_ref, base, plane, grads, rows_out, pairs, cin, cout):
    even, odd = plane_rows(plane, rows_out)
    kept = (rows_out - 1) * pairs
    products = (
        kernel_dot(odd[:kept], grads[pairs:]),
        kernel_dot(even, grads),
        kernel_dot(odd, grads),
    )
    for height_tap in range(3):
        product = products[height_tap]
        start = base + height_tap * 3 * cin
        terms_ref[start : start + cin] = product[cin:, cout:].astype(terms_ref.dtype)
        terms_ref[start + cin : start + 3 * cin] = product[:, :cout].astype(terms_ref.dtype)


def forward_terms(plane, weight, depth_tap, rows_out, pairs):
    even, odd = plane_rows(plane, rows_out)
    lifted = jnp.concatenate([jnp.zeros_like(odd[:pairs]), odd[: (rows_out - 1) * pairs]], axis=0)
    return (
        forward_dot(lifted, tap_weight(weight, depth_tap, 0))
        + forward_dot(even, tap_weight(weight, depth_tap, 1))
        + forward_dot(odd, tap_weight(weight, depth_tap, 2))
    )


def backward_terms(grads, weight, depth_tap, pairs):
    raised = jnp.concatenate([grads[pairs:], jnp.zeros_like(grads[:pairs])], axis=0)
    even = backward_dot(grads, tap_weight(weight, depth_tap, 1))
    odd = backward_dot(grads, tap_weight(weight, depth_tap, 2)) + backward_dot(
        raised, tap_weight(weight, depth_tap, 0)
    )
    return even, odd


def own_kernel(local_ref, grads_ref, terms_ref, plane_ref):
    rows_out, pairs, cout = grads_ref.shape
    cin = local_ref.shape[3] // 2
    grads = with_next_pair(grads_ref[...].reshape(rows_out * pairs, cout), pairs)
    for plane in range(2):
        store_kernel_terms(
            terms_ref, plane * 9 * cin, local_ref[plane], grads, rows_out, pairs, cin, cout
        )
    plane_ref[0] = local_ref[1]


def joined_kernel(core_ref, local_ref, later_ref, terms_ref, kept_ref, sent_ref, scratch_ref):
    rows_out, pairs, cout = later_ref.shape
    cin = local_ref.shape[3] // 2
    count, rows, _ = kept_ref.shape
    total = 27 * cin
    step = -(-total // (2 * count))
    later = with_next_pair(later_ref[...].reshape(rows_out * pairs, cout), pairs)
    store_kernel_terms(scratch_ref, 0, local_ref[1], later, rows_out, pairs, cin, cout)
    scratch_ref[9 * cin : total] = terms_ref[...]
    scratch_ref[total:] = jnp.zeros((scratch_ref.shape[0] - total, cout), jnp.float32)
    first = core_ref[0] == 0
    for index in range(count):
        start = 2 * index * step
        even = scratch_ref[start : start + rows]
        odd = scratch_ref[start + step : start + step + rows]
        kept_ref[index] = jnp.where(first, even, odd)
        sent_ref[index] = jnp.where(first, odd, even)


def merge_kernel(kept_ref, other_ref, chunks_ref):
    chunks_ref[...] = (kept_ref[...] + other_ref[...]).astype(jnp.bfloat16)


def copies_kernel(chunks_ref, copies_ref):
    piece = jnp.sum(chunks_ref[...].astype(jnp.float32), axis=0).astype(jnp.bfloat16)
    for index in range(copies_ref.shape[0]):
        copies_ref[index] = piece


def finish_kernel(
    rim_ref, local_ref, grads_ref, later_ref, weight_ref, output_ref, grad_ref
):
    rows_out, pairs, cout = later_ref.shape
    cells = rows_out * pairs
    grads = with_next_pair(grads_ref[...].reshape(cells, cout), pairs)
    later = with_next_pair(later_ref[...].reshape(cells, cout), pairs)
    total = (
        forward_terms(rim_ref[0], weight_ref, 0, rows_out, pairs)
        + forward_terms(local_ref[0], weight_ref, 1, rows_out, pairs)
        + forward_terms(local_ref[1], weight_ref, 2, rows_out, pairs)
    )
    result = total[:, :cout] + from_previous_pair(total[:, cout:], pairs)
    output_ref[...] = result.astype(jnp.bfloat16).reshape(output_ref.shape)
    spilled = backward_terms(later, weight_ref, 0, pairs)
    own = backward_terms(grads, weight_ref, 2, pairs)
    planes = (
        backward_terms(grads, weight_ref, 1, pairs),
        (spilled[0] + own[0], spilled[1] + own[1]),
    )
    for plane, sides in enumerate(planes):
        for side, values in enumerate(sides):
            rounded = values.astype(jnp.bfloat16)
            for b in range(rows_out):
                grad_ref[plane, 2 * b + side] = rounded[b * pairs : (b + 1) * pairs]


def spread_kernel(step, factor, core_ref, own_ref, other_ref, grad_ref):
    first = core_ref[0] == 0
    for index in range(own_ref.shape[0]):
        own = own_ref[index].astype(jnp.float32) * factor
        other = other_ref[index].astype(jnp.float32) * factor
        for start, block in (
            (2 * index * step, jnp.where(first, own, other)),
            ((2 * index + 1) * step, jnp.where(first, other, own)),
        ):
            valid = min(step, grad_ref.shape[0] - start)
            if valid > 0:
                grad_ref[start : start + valid] = block[:valid]


def swapped(value):
    return lax.ppermute(value, "c", [(0, 1), (1, 0)])


def shards(volume, weight, cotangent):
    local = volume[0]
    grads = cotangent[0, 0]
    rows_out, pairs, cout = grads.shape
    cin = weight.shape[3]
    total = 27 * cin
    cells = rows_out * pairs
    count = math.prod(lax.axis_size(axis) for axis in SLAB)
    step = -(-total // (2 * count))
    rows = -(-step // 16) * 16
    devices = math.prod(lax.axis_size(axis) for axis in DP + SPACE)
    factor = 1.0 / math.sqrt(devices * cells)

    later = passed_along(grads, SPACE, -1)
    terms, plane = pl.pallas_call(
        own_kernel,
        out_shape=(
            jax.ShapeDtypeStruct((18 * cin, cout), jnp.float32),
            jax.ShapeDtypeStruct((1, *local.shape[1:]), jnp.bfloat16),
        ),
        cost_estimate=pl.CostEstimate(flops=300_000_000, bytes_accessed=2_000_000, transcendentals=0),
        compiler_params=pltpu.CompilerParams(vmem_limit_bytes=VMEM_BYTES),
        name="own",
    )(local, grads)
    core = jnp.full((1,), lax.axis_index("c"), jnp.int32)
    in_vmem = pl.BlockSpec(memory_space=pltpu.VMEM)
    in_smem = pl.BlockSpec(memory_space=pltpu.SMEM)
    kept, sent = pl.pallas_call(
        joined_kernel,
        in_specs=[in_smem, in_vmem, in_vmem, in_vmem],
        out_shape=(
            jax.ShapeDtypeStruct((count, rows, cout), jnp.float32),
            jax.ShapeDtypeStruct((count, rows, cout), jnp.float32),
        ),
        scratch_shapes=[pltpu.VMEM((2 * count * step + 16, cout), jnp.float32)],
        cost_estimate=pl.CostEstimate(flops=60_000_000, bytes_accessed=1_000_000, transcendentals=0),
        compiler_params=pltpu.CompilerParams(vmem_limit_bytes=VMEM_BYTES),
        name="joined",
    )(core, local, later, terms)
    chunks = pl.pallas_call(
        merge_kernel,
        out_shape=jax.ShapeDtypeStruct((count, rows, cout), jnp.bfloat16),
        cost_estimate=pl.CostEstimate(flops=500_000, bytes_accessed=1_000_000, transcendentals=0),
        compiler_params=pltpu.CompilerParams(vmem_limit_bytes=VMEM_BYTES),
        name="merge",
    )(kept, swapped(sent))
    lines = math.prod(lax.axis_size(axis) for axis in LINE)
    copies = pl.pallas_call(
        copies_kernel,
        out_shape=jax.ShapeDtypeStruct((lines, rows, cout), jnp.bfloat16),
        cost_estimate=pl.CostEstimate(flops=500_000, bytes_accessed=700_000, transcendentals=0),
        compiler_params=pltpu.CompilerParams(vmem_limit_bytes=VMEM_BYTES),
        name="copies",
    )(exchange(chunks, SLAB))
    copies, plane, later, local, grads = lax.optimization_barrier(
        (copies, plane, later, local, grads)
    )
    rim = passed_along(plane, SPACE, 1)
    piece = jnp.sum(exchange(copies, LINE).astype(jnp.float32), axis=0)

    output, grad_volume = pl.pallas_call(
        finish_kernel,
        out_shape=(
            jax.ShapeDtypeStruct((rows_out, pairs, cout), jnp.bfloat16),
            jax.ShapeDtypeStruct((2, 2 * rows_out, pairs, 2 * cin), jnp.bfloat16),
        ),
        cost_estimate=pl.CostEstimate(flops=400_000_000, bytes_accessed=1_500_000, transcendentals=0),
        compiler_params=pltpu.CompilerParams(vmem_limit_bytes=VMEM_BYTES),
        name="finish",
    )(rim, local, grads, later, weight)
    piece, output, grad_volume = lax.optimization_barrier((piece, output, grad_volume))
    copies = jnp.broadcast_to(piece.astype(jnp.bfloat16)[None], (count, rows, cout))
    gathered = exchange(copies, SLAB)
    grad_weight = pl.pallas_call(
        functools.partial(spread_kernel, step, factor),
        in_specs=[in_smem, in_vmem, in_vmem],
        out_shape=jax.ShapeDtypeStruct((total, cout), jnp.float32),
        compiler_params=pltpu.CompilerParams(vmem_limit_bytes=VMEM_BYTES),
        name="spread_out",
    )(core, gathered, swapped(gathered))
    return (output[None, None], grad_volume[None], grad_weight.reshape(weight.shape))


def solution(mesh):
    fine = jax.sharding.Mesh(mesh.devices.reshape(SIZES), DP + SPACE)
    split = P(DP, SPACE, None, None, None)
    return jax.shard_map(
        shards,
        mesh=fine,
        in_specs=(split, P(), split),
        out_specs=(split, split, P()),
        check_vma=False,
    )
```

```python
import functools
import math

import jax
import jax.numpy as jnp
from jax import lax
from jax.experimental import pallas as pl
from jax.experimental.pallas import tpu as pltpu
from jax.sharding import PartitionSpec as P

DP = ("x", "zh")
SPACE = ("y", "zn", "ze", "c")
SLAB = ("x", "y", "ze", "c")
LINE = ("zh", "zn")
SIZES = (4, 4, 4, 4, 2, 2)
VMEM_BYTES = 16 << 20


def passed_along(value, axes, steps):
    count = math.prod(lax.axis_size(axis) for axis in axes)
    first, last = (max(0, -steps), min(count, count - steps))
    return lax.ppermute(value, axes, [(source, source + steps) for source in range(first, last)])


def sent(value, pairs):
    return lax.ppermute(value, SPACE, pairs)


def exchange(value, axes):
    return lax.all_to_all(value, axes, 0, 0, tiled=True)


def with_next_pair(cells, pairs):
    wide = cells.astype(jnp.float32)
    rows = wide.shape[0]
    row = lax.broadcasted_iota(jnp.int32, wide.shape, 0)
    ahead = jnp.where(row % pairs == pairs - 1, 0.0, pltpu.roll(wide, rows - 1, 0))
    return jnp.concatenate([cells, ahead.astype(jnp.bfloat16)], axis=1)


def from_previous_pair(wide, pairs):
    row = lax.broadcasted_iota(jnp.int32, wide.shape, 0)
    return jnp.where(row % pairs == 0, 0.0, pltpu.roll(wide, 1, 0))


def plane_rows(plane, rows_out):
    even = jnp.concatenate([plane[2 * b] for b in range(rows_out)], axis=0)
    odd = jnp.concatenate([plane[2 * b + 1] for b in range(rows_out)], axis=0)
    return even, odd


def tap_weight(weight, depth_tap, height_tap):
    taps = weight[depth_tap, height_tap]
    pair = jnp.concatenate([taps[1], taps[2]], axis=0)
    left = jnp.concatenate([jnp.zeros_like(taps[0]), taps[0]], axis=0)
    return jnp.concatenate([pair, left], axis=1)


def forward_dot(rows, weight):
    return lax.dot_general(
        rows, weight, (((1,), (0,)), ((), ())), preferred_element_type=jnp.float32
    )


def backward_dot(rows, weight):
    return lax.dot_general(
        rows, weight, (((1,), (1,)), ((), ())), preferred_element_type=jnp.float32
    )


def kernel_dot(rows, grads):
    return lax.dot_general(
        rows, grads, (((0,), (0,)), ((), ())), preferred_element_type=jnp.float32
    )


def kernel_terms(plane, grads, rows_out, pairs):
    even, odd = plane_rows(plane, rows_out)
    kept = (rows_out - 1) * pairs
    return (
        kernel_dot(odd[:kept], grads[pairs:]),
        kernel_dot(even, grads),
        kernel_dot(odd, grads),
    )


def store_kernel_terms(terms_ref, base, products, cin, cout):
    for height_tap in range(3):
        product = products[height_tap]
        start = base + height_tap * 3 * cin
        terms_ref[start : start + cin] = product[cin:, cout:]
        terms_ref[start + cin : start + 3 * cin] = product[:, :cout]


def forward_terms(plane, weight, depth_tap, rows_out, pairs):
    even, odd = plane_rows(plane, rows_out)
    lifted = jnp.concatenate([jnp.zeros_like(odd[:pairs]), odd[: (rows_out - 1) * pairs]], axis=0)
    return (
        forward_dot(lifted, tap_weight(weight, depth_tap, 0))
        + forward_dot(even, tap_weight(weight, depth_tap, 1))
        + forward_dot(odd, tap_weight(weight, depth_tap, 2))
    )


def backward_terms(grads, weight, depth_tap, pairs):
    raised = jnp.concatenate([grads[pairs:], jnp.zeros_like(grads[:pairs])], axis=0)
    even = backward_dot(grads, tap_weight(weight, depth_tap, 1))
    odd = backward_dot(grads, tap_weight(weight, depth_tap, 2)) + backward_dot(
        raised, tap_weight(weight, depth_tap, 0)
    )
    return even, odd


def own_kernel(local_ref, grads_ref, terms_ref, plane_ref):
    rows_out, pairs, cout = grads_ref.shape
    cin = local_ref.shape[3] // 2
    grads = with_next_pair(grads_ref[...].reshape(rows_out * pairs, cout), pairs)
    for plane in range(2):
        products = kernel_terms(local_ref[plane], grads, rows_out, pairs)
        store_kernel_terms(terms_ref, plane * 9 * cin, products, cin, cout)
    plane_ref[0] = local_ref[1]


def joined_kernel(
    local_ref, later_ref, far_plane_ref, far_grads_ref, terms_ref, chunks_ref, scratch_ref
):
    rows_out, pairs, cout = later_ref.shape
    cin = local_ref.shape[3] // 2
    count, rows, _ = chunks_ref.shape
    total = 27 * cin
    step = total // count
    later = with_next_pair(later_ref[...].reshape(rows_out * pairs, cout), pairs)
    far = with_next_pair(far_grads_ref[...].reshape(rows_out * pairs, cout), pairs)
    near_terms = kernel_terms(local_ref[1], later, rows_out, pairs)
    far_terms = kernel_terms(far_plane_ref[0], far, rows_out, pairs)
    products = [near + other for near, other in zip(near_terms, far_terms)]
    store_kernel_terms(scratch_ref, 0, products, cin, cout)
    scratch_ref[9 * cin : total] = terms_ref[...]
    scratch_ref[total:] = jnp.zeros((scratch_ref.shape[0] - total, cout), jnp.float32)
    for index in range(count):
        chunks_ref[index] = scratch_ref[index * step : index * step + rows].astype(jnp.bfloat16)


def copies_kernel(chunks_ref, copies_ref):
    piece = jnp.sum(chunks_ref[...].astype(jnp.float32), axis=0).astype(jnp.bfloat16)
    for index in range(copies_ref.shape[0]):
        copies_ref[index] = piece


def finish_kernel(
    rim_ref, local_ref, grads_ref, later_ref, after_ref, weight_ref, output_ref, grad_ref
):
    rows_out, pairs, cout = later_ref.shape
    cells = rows_out * pairs
    grads = with_next_pair(grads_ref[...].reshape(cells, cout), pairs)
    later = with_next_pair((later_ref[...] + after_ref[...]).reshape(cells, cout), pairs)
    total = (
        forward_terms(rim_ref[0], weight_ref, 0, rows_out, pairs)
        + forward_terms(local_ref[0], weight_ref, 1, rows_out, pairs)
        + forward_terms(local_ref[1], weight_ref, 2, rows_out, pairs)
    )
    result = total[:, :cout] + from_previous_pair(total[:, cout:], pairs)
    output_ref[...] = result.astype(jnp.bfloat16).reshape(output_ref.shape)
    spilled = backward_terms(later, weight_ref, 0, pairs)
    own = backward_terms(grads, weight_ref, 2, pairs)
    planes = (
        backward_terms(grads, weight_ref, 1, pairs),
        (spilled[0] + own[0], spilled[1] + own[1]),
    )
    for plane, sides in enumerate(planes):
        for side, values in enumerate(sides):
            rounded = values.astype(jnp.bfloat16)
            for b in range(rows_out):
                grad_ref[plane, 2 * b + side] = rounded[b * pairs : (b + 1) * pairs]


def spread_kernel(step, factor, chunks_ref, grad_ref):
    for index in range(chunks_ref.shape[0]):
        block = chunks_ref[index].astype(jnp.float32)[:step]
        grad_ref[index * step : (index + 1) * step] = block * factor


def shards(volume, weight, cotangent):
    local = volume[0]
    grads = cotangent[0, 0]
    rows_out, pairs, cout = grads.shape
    cin = weight.shape[3]
    total = 27 * cin
    cells = rows_out * pairs
    count = math.prod(lax.axis_size(axis) for axis in SLAB)
    step = total // count
    rows = -(-step // 16) * 16
    devices = math.prod(lax.axis_size(axis) for axis in DP + SPACE)
    factor = 1.0 / math.sqrt(devices * cells)

    places = math.prod(lax.axis_size(axis) for axis in SPACE)
    run = places // lax.axis_size("y")
    bends = range(run, places, run)
    far_grads = sent(grads, [(place, place + run // 2) for place in bends])
    far_plane = sent(local[1:2], [(place - 1, place + run // 2) for place in bends])
    later = sent(grads, [(place, place - 1) for place in range(1, places) if place % run])
    terms, plane = pl.pallas_call(
        own_kernel,
        out_shape=(
            jax.ShapeDtypeStruct((18 * cin, cout), jnp.float32),
            jax.ShapeDtypeStruct((1, *local.shape[1:]), jnp.bfloat16),
        ),
        cost_estimate=pl.CostEstimate(flops=300_000_000, bytes_accessed=2_000_000, transcendentals=0),
        compiler_params=pltpu.CompilerParams(vmem_limit_bytes=VMEM_BYTES),
        name="own",
    )(local, grads)
    chunks = pl.pallas_call(
        joined_kernel,
        out_shape=jax.ShapeDtypeStruct((count, rows, cout), jnp.bfloat16),
        scratch_shapes=[pltpu.VMEM((total + 16, cout), jnp.float32)],
        cost_estimate=pl.CostEstimate(flops=60_000_000, bytes_accessed=1_000_000, transcendentals=0),
        compiler_params=pltpu.CompilerParams(vmem_limit_bytes=VMEM_BYTES),
        name="joined",
    )(local, later, far_plane, far_grads, terms)
    lines = math.prod(lax.axis_size(axis) for axis in LINE)
    copies = pl.pallas_call(
        copies_kernel,
        out_shape=jax.ShapeDtypeStruct((lines, rows, cout), jnp.bfloat16),
        cost_estimate=pl.CostEstimate(flops=500_000, bytes_accessed=700_000, transcendentals=0),
        compiler_params=pltpu.CompilerParams(vmem_limit_bytes=VMEM_BYTES),
        name="copies",
    )(exchange(chunks, SLAB))
    copies, plane, later, local, grads = lax.optimization_barrier(
        (copies, plane, later, local, grads)
    )
    rim = passed_along(plane, SPACE, 1)
    after = sent(grads, [(place, place - 1) for place in bends])
    piece = jnp.sum(exchange(copies, LINE).astype(jnp.float32), axis=0)

    output, grad_volume = pl.pallas_call(
        finish_kernel,
        out_shape=(
            jax.ShapeDtypeStruct((rows_out, pairs, cout), jnp.bfloat16),
            jax.ShapeDtypeStruct((2, 2 * rows_out, pairs, 2 * cin), jnp.bfloat16),
        ),
        cost_estimate=pl.CostEstimate(flops=400_000_000, bytes_accessed=1_500_000, transcendentals=0),
        compiler_params=pltpu.CompilerParams(vmem_limit_bytes=VMEM_BYTES),
        name="finish",
    )(rim, local, grads, later, after, weight)
    piece, output, grad_volume = lax.optimization_barrier((piece, output, grad_volume))
    copies = jnp.broadcast_to(piece.astype(jnp.bfloat16)[None], (count, rows, cout))
    gathered = exchange(copies, SLAB)
    grad_weight = pl.pallas_call(
        functools.partial(spread_kernel, step, factor),
        out_shape=jax.ShapeDtypeStruct((total, cout), jnp.float32),
        compiler_params=pltpu.CompilerParams(vmem_limit_bytes=VMEM_BYTES),
        name="spread_out",
    )(gathered)
    return (output[None, None], grad_volume[None], grad_weight.reshape(weight.shape))


def solution(mesh):
    fine = jax.sharding.Mesh(mesh.devices.reshape(SIZES), DP + SPACE)
    split = P(DP, SPACE, None, None, None)
    return jax.shard_map(
        shards,
        mesh=fine,
        in_specs=(split, P(), split),
        out_specs=(split, split, P()),
        check_vma=False,
    )
```

```python
import functools
import math

import jax
import jax.numpy as jnp
from jax import lax
from jax.experimental import pallas as pl
from jax.experimental.pallas import tpu as pltpu
from jax.sharding import PartitionSpec as P

DP = ("x", "zh")
SPACE = ("y", "zn", "ze", "c")
SLAB = ("c", "ze", "y", "x")
LINE = ("zn", "zh")
SIZES = (4, 4, 4, 4, 2, 2)
VMEM_BYTES = 16 << 20


def passed_along(value, axes, steps):
    count = math.prod(lax.axis_size(axis) for axis in axes)
    first, last = (max(0, -steps), min(count, count - steps))
    return lax.ppermute(value, axes, [(source, source + steps) for source in range(first, last)])


def exchange(value, axes):
    return lax.all_to_all(value, axes, 0, 0, tiled=True)


def with_next_pair(cells, pairs):
    wide = cells.astype(jnp.float32)
    rows = wide.shape[0]
    row = lax.broadcasted_iota(jnp.int32, wide.shape, 0)
    ahead = jnp.where(row % pairs == pairs - 1, 0.0, pltpu.roll(wide, rows - 1, 0))
    return jnp.concatenate([cells, ahead.astype(jnp.bfloat16)], axis=1)


def from_previous_pair(wide, pairs):
    row = lax.broadcasted_iota(jnp.int32, wide.shape, 0)
    return jnp.where(row % pairs == 0, 0.0, pltpu.roll(wide, 1, 0))


def plane_rows(plane, rows_out):
    even = jnp.concatenate([plane[2 * b] for b in range(rows_out)], axis=0)
    odd = jnp.concatenate([plane[2 * b + 1] for b in range(rows_out)], axis=0)
    return even, odd


def tap_weight(weight, depth_tap, height_tap):
    taps = weight[depth_tap, height_tap]
    pair = jnp.concatenate([taps[1], taps[2]], axis=0)
    left = jnp.concatenate([jnp.zeros_like(taps[0]), taps[0]], axis=0)
    return jnp.concatenate([pair, left], axis=1)


def forward_dot(rows, weight):
    return lax.dot_general(
        rows, weight, (((1,), (0,)), ((), ())), preferred_element_type=jnp.float32
    )


def backward_dot(rows, weight):
    return lax.dot_general(
        rows, weight, (((1,), (1,)), ((), ())), preferred_element_type=jnp.float32
    )


def kernel_dot(rows, grads):
    return lax.dot_general(
        rows, grads, (((0,), (0,)), ((), ())), preferred_element_type=jnp.float32
    )


def store_kernel_terms(terms_ref, base, plane, grads, rows_out, pairs, cin, cout):
    even, odd = plane_rows(plane, rows_out)
    kept = (rows_out - 1) * pairs
    products = (
        kernel_dot(odd[:kept], grads[pairs:]),
        kernel_dot(even, grads),
        kernel_dot(odd, grads),
    )
    for height_tap in range(3):
        product = products[height_tap]
        start = base + height_tap * 3 * cin
        terms_ref[start : start + cin] = product[cin:, cout:].astype(terms_ref.dtype)
        terms_ref[start + cin : start + 3 * cin] = product[:, :cout].astype(terms_ref.dtype)


def forward_terms(plane, weight, depth_tap, rows_out, pairs):
    even, odd = plane_rows(plane, rows_out)
    lifted = jnp.concatenate([jnp.zeros_like(odd[:pairs]), odd[: (rows_out - 1) * pairs]], axis=0)
    return (
        forward_dot(lifted, tap_weight(weight, depth_tap, 0))
        + forward_dot(even, tap_weight(weight, depth_tap, 1))
        + forward_dot(odd, tap_weight(weight, depth_tap, 2))
    )


def backward_terms(grads, weight, depth_tap, pairs):
    raised = jnp.concatenate([grads[pairs:], jnp.zeros_like(grads[:pairs])], axis=0)
    even = backward_dot(grads, tap_weight(weight, depth_tap, 1))
    odd = backward_dot(grads, tap_weight(weight, depth_tap, 2)) + backward_dot(
        raised, tap_weight(weight, depth_tap, 0)
    )
    return even, odd


def own_kernel(local_ref, grads_ref, terms_ref, plane_ref):
    rows_out, pairs, cout = grads_ref.shape
    cin = local_ref.shape[3] // 2
    grads = with_next_pair(grads_ref[...].reshape(rows_out * pairs, cout), pairs)
    for plane in range(2):
        store_kernel_terms(
            terms_ref, plane * 9 * cin, local_ref[plane], grads, rows_out, pairs, cin, cout
        )
    plane_ref[0] = local_ref[1]


def joined_kernel(local_ref, later_ref, terms_ref, chunks_ref, scratch_ref):
    rows_out, pairs, cout = later_ref.shape
    cin = local_ref.shape[3] // 2
    count, rows, _ = chunks_ref.shape
    total = 27 * cin
    step = total // count
    later = with_next_pair(later_ref[...].reshape(rows_out * pairs, cout), pairs)
    store_kernel_terms(scratch_ref, 0, local_ref[1], later, rows_out, pairs, cin, cout)
    scratch_ref[9 * cin : total] = terms_ref[...]
    scratch_ref[total:] = jnp.zeros((scratch_ref.shape[0] - total, cout), jnp.float32)
    for index in range(count):
        chunks_ref[index] = scratch_ref[index * step : index * step + rows].astype(jnp.bfloat16)


def copies_kernel(chunks_ref, copies_ref):
    piece = jnp.sum(chunks_ref[...].astype(jnp.float32), axis=0).astype(jnp.bfloat16)
    for index in range(copies_ref.shape[0]):
        copies_ref[index] = piece


def finish_kernel(
    rim_ref, local_ref, grads_ref, later_ref, weight_ref, output_ref, grad_ref
):
    rows_out, pairs, cout = later_ref.shape
    cells = rows_out * pairs
    grads = with_next_pair(grads_ref[...].reshape(cells, cout), pairs)
    later = with_next_pair(later_ref[...].reshape(cells, cout), pairs)
    total = (
        forward_terms(rim_ref[0], weight_ref, 0, rows_out, pairs)
        + forward_terms(local_ref[0], weight_ref, 1, rows_out, pairs)
        + forward_terms(local_ref[1], weight_ref, 2, rows_out, pairs)
    )
    result = total[:, :cout] + from_previous_pair(total[:, cout:], pairs)
    output_ref[...] = result.astype(jnp.bfloat16).reshape(output_ref.shape)
    spilled = backward_terms(later, weight_ref, 0, pairs)
    own = backward_terms(grads, weight_ref, 2, pairs)
    planes = (
        backward_terms(grads, weight_ref, 1, pairs),
        (spilled[0] + own[0], spilled[1] + own[1]),
    )
    for plane, sides in enumerate(planes):
        for side, values in enumerate(sides):
            rounded = values.astype(jnp.bfloat16)
            for b in range(rows_out):
                grad_ref[plane, 2 * b + side] = rounded[b * pairs : (b + 1) * pairs]


def spread_kernel(step, factor, chunks_ref, grad_ref):
    for index in range(chunks_ref.shape[0]):
        block = chunks_ref[index].astype(jnp.float32)[:step]
        grad_ref[index * step : (index + 1) * step] = block * factor


def shards(volume, weight, cotangent):
    local = volume[0]
    grads = cotangent[0, 0]
    rows_out, pairs, cout = grads.shape
    cin = weight.shape[3]
    total = 27 * cin
    cells = rows_out * pairs
    count = math.prod(lax.axis_size(axis) for axis in SLAB)
    step = total // count
    rows = -(-step // 16) * 16
    devices = math.prod(lax.axis_size(axis) for axis in DP + SPACE)
    factor = 1.0 / math.sqrt(devices * cells)

    later = passed_along(grads, SPACE, -1)
    terms, plane = pl.pallas_call(
        own_kernel,
        out_shape=(
            jax.ShapeDtypeStruct((18 * cin, cout), jnp.float32),
            jax.ShapeDtypeStruct((1, *local.shape[1:]), jnp.bfloat16),
        ),
        cost_estimate=pl.CostEstimate(flops=300_000_000, bytes_accessed=2_000_000, transcendentals=0),
        compiler_params=pltpu.CompilerParams(vmem_limit_bytes=VMEM_BYTES),
        name="own",
    )(local, grads)
    chunks = pl.pallas_call(
        joined_kernel,
        out_shape=jax.ShapeDtypeStruct((count, rows, cout), jnp.bfloat16),
        scratch_shapes=[pltpu.VMEM((total + 16, cout), jnp.float32)],
        cost_estimate=pl.CostEstimate(flops=60_000_000, bytes_accessed=1_000_000, transcendentals=0),
        compiler_params=pltpu.CompilerParams(vmem_limit_bytes=VMEM_BYTES),
        name="joined",
    )(local, later, terms)
    lines = math.prod(lax.axis_size(axis) for axis in LINE)
    copies = pl.pallas_call(
        copies_kernel,
        out_shape=jax.ShapeDtypeStruct((lines, rows, cout), jnp.bfloat16),
        cost_estimate=pl.CostEstimate(flops=500_000, bytes_accessed=700_000, transcendentals=0),
        compiler_params=pltpu.CompilerParams(vmem_limit_bytes=VMEM_BYTES),
        name="copies",
    )(exchange(chunks, SLAB))
    copies, plane, later, local, grads = lax.optimization_barrier(
        (copies, plane, later, local, grads)
    )
    rim = passed_along(plane, SPACE, 1)
    piece = jnp.sum(exchange(copies, LINE).astype(jnp.float32), axis=0)

    output, grad_volume = pl.pallas_call(
        finish_kernel,
        out_shape=(
            jax.ShapeDtypeStruct((rows_out, pairs, cout), jnp.bfloat16),
            jax.ShapeDtypeStruct((2, 2 * rows_out, pairs, 2 * cin), jnp.bfloat16),
        ),
        cost_estimate=pl.CostEstimate(flops=400_000_000, bytes_accessed=1_500_000, transcendentals=0),
        compiler_params=pltpu.CompilerParams(vmem_limit_bytes=VMEM_BYTES),
        name="finish",
    )(rim, local, grads, later, weight)
    piece, output, grad_volume = lax.optimization_barrier((piece, output, grad_volume))
    copies = jnp.broadcast_to(piece.astype(jnp.bfloat16)[None], (count, rows, cout))
    gathered = exchange(copies, SLAB)
    grad_weight = pl.pallas_call(
        functools.partial(spread_kernel, step, factor),
        out_shape=jax.ShapeDtypeStruct((total, cout), jnp.float32),
        compiler_params=pltpu.CompilerParams(vmem_limit_bytes=VMEM_BYTES),
        name="spread_out",
    )(gathered)
    return (output[None, None], grad_volume[None], grad_weight.reshape(weight.shape))


def solution(mesh):
    fine = jax.sharding.Mesh(mesh.devices.reshape(SIZES), DP + SPACE)
    split = P(DP, SPACE, None, None, None)
    return jax.shard_map(
        shards,
        mesh=fine,
        in_specs=(split, P(), split),
        out_specs=(split, split, P()),
        check_vma=False,
    )
```

```python
import functools
import math

import jax
import jax.numpy as jnp
from jax import lax
from jax.experimental import pallas as pl
from jax.experimental.pallas import tpu as pltpu
from jax.sharding import PartitionSpec as P

DP = ("x", "zh")
SPACE = ("y", "zn", "ze", "c")
SLAB = ("c", "ze", "y", "x")
LINE = ("zn", "zh")
SIZES = (4, 4, 4, 4, 2, 2)
VMEM_BYTES = 16 << 20


def passed_along(value, axes, steps):
    count = math.prod(lax.axis_size(axis) for axis in axes)
    first, last = (max(0, -steps), min(count, count - steps))
    return lax.ppermute(value, axes, [(source, source + steps) for source in range(first, last)])


def sent(value, pairs):
    return lax.ppermute(value, SPACE, pairs)


def exchange(value, axes):
    return lax.all_to_all(value, axes, 0, 0, tiled=True)


def with_next_pair(cells, pairs):
    wide = cells.astype(jnp.float32)
    rows = wide.shape[0]
    row = lax.broadcasted_iota(jnp.int32, wide.shape, 0)
    ahead = jnp.where(row % pairs == pairs - 1, 0.0, pltpu.roll(wide, rows - 1, 0))
    return jnp.concatenate([cells, ahead.astype(jnp.bfloat16)], axis=1)


def from_previous_pair(wide, pairs):
    row = lax.broadcasted_iota(jnp.int32, wide.shape, 0)
    return jnp.where(row % pairs == 0, 0.0, pltpu.roll(wide, 1, 0))


def plane_rows(plane, rows_out):
    even = jnp.concatenate([plane[2 * b] for b in range(rows_out)], axis=0)
    odd = jnp.concatenate([plane[2 * b + 1] for b in range(rows_out)], axis=0)
    return even, odd


def tap_weight(weight, depth_tap, height_tap):
    taps = weight[depth_tap, height_tap]
    pair = jnp.concatenate([taps[1], taps[2]], axis=0)
    left = jnp.concatenate([jnp.zeros_like(taps[0]), taps[0]], axis=0)
    return jnp.concatenate([pair, left], axis=1)


def forward_dot(rows, weight):
    return lax.dot_general(
        rows, weight, (((1,), (0,)), ((), ())), preferred_element_type=jnp.float32
    )


def backward_dot(rows, weight):
    return lax.dot_general(
        rows, weight, (((1,), (1,)), ((), ())), preferred_element_type=jnp.float32
    )


def kernel_dot(rows, grads):
    return lax.dot_general(
        rows, grads, (((0,), (0,)), ((), ())), preferred_element_type=jnp.float32
    )


def kernel_terms(plane, grads, rows_out, pairs):
    even, odd = plane_rows(plane, rows_out)
    kept = (rows_out - 1) * pairs
    return (
        kernel_dot(odd[:kept], grads[pairs:]),
        kernel_dot(even, grads),
        kernel_dot(odd, grads),
    )


def store_kernel_terms(terms_ref, base, products, cin, cout):
    for height_tap in range(3):
        product = products[height_tap]
        start = base + height_tap * 3 * cin
        terms_ref[start : start + cin] = product[cin:, cout:]
        terms_ref[start + cin : start + 3 * cin] = product[:, :cout]


def forward_terms(plane, weight, depth_tap, rows_out, pairs):
    even, odd = plane_rows(plane, rows_out)
    lifted = jnp.concatenate([jnp.zeros_like(odd[:pairs]), odd[: (rows_out - 1) * pairs]], axis=0)
    return (
        forward_dot(lifted, tap_weight(weight, depth_tap, 0))
        + forward_dot(even, tap_weight(weight, depth_tap, 1))
        + forward_dot(odd, tap_weight(weight, depth_tap, 2))
    )


def backward_terms(grads, weight, depth_tap, pairs):
    raised = jnp.concatenate([grads[pairs:], jnp.zeros_like(grads[:pairs])], axis=0)
    even = backward_dot(grads, tap_weight(weight, depth_tap, 1))
    odd = backward_dot(grads, tap_weight(weight, depth_tap, 2)) + backward_dot(
        raised, tap_weight(weight, depth_tap, 0)
    )
    return even, odd


def own_kernel(local_ref, grads_ref, terms_ref, plane_ref):
    rows_out, pairs, cout = grads_ref.shape
    cin = local_ref.shape[3] // 2
    grads = with_next_pair(grads_ref[...].reshape(rows_out * pairs, cout), pairs)
    for plane in range(2):
        products = kernel_terms(local_ref[plane], grads, rows_out, pairs)
        store_kernel_terms(terms_ref, plane * 9 * cin, products, cin, cout)
    plane_ref[0] = local_ref[1]


def joined_kernel(
    local_ref, later_ref, far_plane_ref, far_grads_ref, terms_ref, chunks_ref, scratch_ref
):
    rows_out, pairs, cout = later_ref.shape
    cin = local_ref.shape[3] // 2
    count, rows, _ = chunks_ref.shape
    total = 27 * cin
    step = total // count
    later = with_next_pair(later_ref[...].reshape(rows_out * pairs, cout), pairs)
    far = with_next_pair(far_grads_ref[...].reshape(rows_out * pairs, cout), pairs)
    near_terms = kernel_terms(local_ref[1], later, rows_out, pairs)
    far_terms = kernel_terms(far_plane_ref[0], far, rows_out, pairs)
    products = [near + other for near, other in zip(near_terms, far_terms)]
    store_kernel_terms(scratch_ref, 0, products, cin, cout)
    scratch_ref[9 * cin : total] = terms_ref[...]
    scratch_ref[total:] = jnp.zeros((scratch_ref.shape[0] - total, cout), jnp.float32)
    for index in range(count):
        chunks_ref[index] = scratch_ref[index * step : index * step + rows].astype(jnp.bfloat16)


def copies_kernel(chunks_ref, copies_ref):
    piece = jnp.sum(chunks_ref[...].astype(jnp.float32), axis=0).astype(jnp.bfloat16)
    for index in range(copies_ref.shape[0]):
        copies_ref[index] = piece


def finish_kernel(
    rim_ref, local_ref, grads_ref, later_ref, after_ref, weight_ref, output_ref, grad_ref
):
    rows_out, pairs, cout = later_ref.shape
    cells = rows_out * pairs
    grads = with_next_pair(grads_ref[...].reshape(cells, cout), pairs)
    later = with_next_pair((later_ref[...] + after_ref[...]).reshape(cells, cout), pairs)
    total = (
        forward_terms(rim_ref[0], weight_ref, 0, rows_out, pairs)
        + forward_terms(local_ref[0], weight_ref, 1, rows_out, pairs)
        + forward_terms(local_ref[1], weight_ref, 2, rows_out, pairs)
    )
    result = total[:, :cout] + from_previous_pair(total[:, cout:], pairs)
    output_ref[...] = result.astype(jnp.bfloat16).reshape(output_ref.shape)
    spilled = backward_terms(later, weight_ref, 0, pairs)
    own = backward_terms(grads, weight_ref, 2, pairs)
    planes = (
        backward_terms(grads, weight_ref, 1, pairs),
        (spilled[0] + own[0], spilled[1] + own[1]),
    )
    for plane, sides in enumerate(planes):
        for side, values in enumerate(sides):
            rounded = values.astype(jnp.bfloat16)
            for b in range(rows_out):
                grad_ref[plane, 2 * b + side] = rounded[b * pairs : (b + 1) * pairs]


def spread_kernel(step, factor, chunks_ref, grad_ref):
    for index in range(chunks_ref.shape[0]):
        block = chunks_ref[index].astype(jnp.float32)[:step]
        grad_ref[index * step : (index + 1) * step] = block * factor


def shards(volume, weight, cotangent):
    local = volume[0]
    grads = cotangent[0, 0]
    rows_out, pairs, cout = grads.shape
    cin = weight.shape[3]
    total = 27 * cin
    cells = rows_out * pairs
    count = math.prod(lax.axis_size(axis) for axis in SLAB)
    step = total // count
    rows = -(-step // 16) * 16
    devices = math.prod(lax.axis_size(axis) for axis in DP + SPACE)
    factor = 1.0 / math.sqrt(devices * cells)

    places = math.prod(lax.axis_size(axis) for axis in SPACE)
    run = places // lax.axis_size("y")
    bends = range(run, places, run)
    far_grads = sent(grads, [(place, place + run // 2) for place in bends])
    far_plane = sent(local[1:2], [(place - 1, place + run // 2) for place in bends])
    later = sent(grads, [(place, place - 1) for place in range(1, places) if place % run])
    terms, plane = pl.pallas_call(
        own_kernel,
        out_shape=(
            jax.ShapeDtypeStruct((18 * cin, cout), jnp.float32),
            jax.ShapeDtypeStruct((1, *local.shape[1:]), jnp.bfloat16),
        ),
        cost_estimate=pl.CostEstimate(flops=300_000_000, bytes_accessed=2_000_000, transcendentals=0),
        compiler_params=pltpu.CompilerParams(vmem_limit_bytes=VMEM_BYTES),
        name="own",
    )(local, grads)
    chunks = pl.pallas_call(
        joined_kernel,
        out_shape=jax.ShapeDtypeStruct((count, rows, cout), jnp.bfloat16),
        scratch_shapes=[pltpu.VMEM((total + 16, cout), jnp.float32)],
        cost_estimate=pl.CostEstimate(flops=60_000_000, bytes_accessed=1_000_000, transcendentals=0),
        compiler_params=pltpu.CompilerParams(vmem_limit_bytes=VMEM_BYTES),
        name="joined",
    )(local, later, far_plane, far_grads, terms)
    lines = math.prod(lax.axis_size(axis) for axis in LINE)
    copies = pl.pallas_call(
        copies_kernel,
        out_shape=jax.ShapeDtypeStruct((lines, rows, cout), jnp.bfloat16),
        cost_estimate=pl.CostEstimate(flops=500_000, bytes_accessed=700_000, transcendentals=0),
        compiler_params=pltpu.CompilerParams(vmem_limit_bytes=VMEM_BYTES),
        name="copies",
    )(exchange(chunks, SLAB))
    copies, plane, later, local, grads = lax.optimization_barrier(
        (copies, plane, later, local, grads)
    )
    rim = passed_along(plane, SPACE, 1)
    after = sent(grads, [(place, place - 1) for place in bends])
    piece = jnp.sum(exchange(copies, LINE).astype(jnp.float32), axis=0)

    output, grad_volume = pl.pallas_call(
        finish_kernel,
        out_shape=(
            jax.ShapeDtypeStruct((rows_out, pairs, cout), jnp.bfloat16),
            jax.ShapeDtypeStruct((2, 2 * rows_out, pairs, 2 * cin), jnp.bfloat16),
        ),
        cost_estimate=pl.CostEstimate(flops=400_000_000, bytes_accessed=1_500_000, transcendentals=0),
        compiler_params=pltpu.CompilerParams(vmem_limit_bytes=VMEM_BYTES),
        name="finish",
    )(rim, local, grads, later, after, weight)
    piece, output, grad_volume = lax.optimization_barrier((piece, output, grad_volume))
    copies = jnp.broadcast_to(piece.astype(jnp.bfloat16)[None], (count, rows, cout))
    gathered = exchange(copies, SLAB)
    grad_weight = pl.pallas_call(
        functools.partial(spread_kernel, step, factor),
        out_shape=jax.ShapeDtypeStruct((total, cout), jnp.float32),
        compiler_params=pltpu.CompilerParams(vmem_limit_bytes=VMEM_BYTES),
        name="spread_out",
    )(gathered)
    return (output[None, None], grad_volume[None], grad_weight.reshape(weight.shape))


def solution(mesh):
    fine = jax.sharding.Mesh(mesh.devices.reshape(SIZES), DP + SPACE)
    split = P(DP, SPACE, None, None, None)
    return jax.shard_map(
        shards,
        mesh=fine,
        in_specs=(split, P(), split),
        out_specs=(split, split, P()),
        check_vma=False,
    )
```

```python
import functools
import math

import jax
import jax.numpy as jnp
from jax import lax
from jax.experimental import pallas as pl
from jax.experimental.pallas import tpu as pltpu
from jax.sharding import PartitionSpec as P

DP = ("x", "zh")
SPACE = ("y", "zn", "ze", "c")
SLAB = ("c", "ze", "y", "x")
LINE = ("zn", "zh")
SIZES = (4, 4, 4, 4, 2, 2)
VMEM_BYTES = 16 << 20


def passed_along(value, axes, steps):
    count = math.prod(lax.axis_size(axis) for axis in axes)
    first, last = (max(0, -steps), min(count, count - steps))
    return lax.ppermute(value, axes, [(source, source + steps) for source in range(first, last)])


def exchange(value, axes):
    return lax.all_to_all(value, axes, 0, 0, tiled=True)


def with_next_pair(cells, pairs):
    wide = cells.astype(jnp.float32)
    rows = wide.shape[0]
    row = lax.broadcasted_iota(jnp.int32, wide.shape, 0)
    ahead = jnp.where(row % pairs == pairs - 1, 0.0, pltpu.roll(wide, rows - 1, 0))
    return jnp.concatenate([cells, ahead.astype(jnp.bfloat16)], axis=1)


def from_previous_pair(wide, pairs):
    row = lax.broadcasted_iota(jnp.int32, wide.shape, 0)
    return jnp.where(row % pairs == 0, 0.0, pltpu.roll(wide, 1, 0))


def plane_rows(plane, rows_out):
    even = jnp.concatenate([plane[2 * b] for b in range(rows_out)], axis=0)
    odd = jnp.concatenate([plane[2 * b + 1] for b in range(rows_out)], axis=0)
    return even, odd


def tap_weight(weight, depth_tap, height_tap):
    taps = weight[depth_tap, height_tap]
    pair = jnp.concatenate([taps[1], taps[2]], axis=0)
    left = jnp.concatenate([jnp.zeros_like(taps[0]), taps[0]], axis=0)
    return jnp.concatenate([pair, left], axis=1)


def forward_dot(rows, weight):
    return lax.dot_general(
        rows, weight, (((1,), (0,)), ((), ())), preferred_element_type=jnp.float32
    )


def backward_dot(rows, weight):
    return lax.dot_general(
        rows, weight, (((1,), (1,)), ((), ())), preferred_element_type=jnp.float32
    )


def kernel_dot(rows, grads):
    return lax.dot_general(
        rows, grads, (((0,), (0,)), ((), ())), preferred_element_type=jnp.float32
    )


def store_kernel_terms(terms_ref, base, plane, grads, rows_out, pairs, cin, cout):
    even, odd = plane_rows(plane, rows_out)
    kept = (rows_out - 1) * pairs
    products = (
        kernel_dot(odd[:kept], grads[pairs:]),
        kernel_dot(even, grads),
        kernel_dot(odd, grads),
    )
    for height_tap in range(3):
        product = products[height_tap]
        start = base + height_tap * 3 * cin
        terms_ref[start : start + cin] = product[cin:, cout:].astype(terms_ref.dtype)
        terms_ref[start + cin : start + 3 * cin] = product[:, :cout].astype(terms_ref.dtype)


def forward_terms(plane, weight, depth_tap, rows_out, pairs):
    even, odd = plane_rows(plane, rows_out)
    lifted = jnp.concatenate([jnp.zeros_like(odd[:pairs]), odd[: (rows_out - 1) * pairs]], axis=0)
    return (
        forward_dot(lifted, tap_weight(weight, depth_tap, 0))
        + forward_dot(even, tap_weight(weight, depth_tap, 1))
        + forward_dot(odd, tap_weight(weight, depth_tap, 2))
    )


def backward_terms(grads, weight, depth_tap, pairs):
    raised = jnp.concatenate([grads[pairs:], jnp.zeros_like(grads[:pairs])], axis=0)
    even = backward_dot(grads, tap_weight(weight, depth_tap, 1))
    odd = backward_dot(grads, tap_weight(weight, depth_tap, 2)) + backward_dot(
        raised, tap_weight(weight, depth_tap, 0)
    )
    return even, odd


def own_kernel(local_ref, grads_ref, terms_ref, plane_ref):
    rows_out, pairs, cout = grads_ref.shape
    cin = local_ref.shape[3] // 2
    grads = with_next_pair(grads_ref[...].reshape(rows_out * pairs, cout), pairs)
    for plane in range(2):
        store_kernel_terms(
            terms_ref, plane * 9 * cin, local_ref[plane], grads, rows_out, pairs, cin, cout
        )
    plane_ref[0] = local_ref[1]


def joined_kernel(local_ref, later_ref, terms_ref, chunks_ref, scratch_ref):
    rows_out, pairs, cout = later_ref.shape
    cin = local_ref.shape[3] // 2
    count, rows, _ = chunks_ref.shape
    total = 27 * cin
    step = total // count
    later = with_next_pair(later_ref[...].reshape(rows_out * pairs, cout), pairs)
    store_kernel_terms(scratch_ref, 0, local_ref[1], later, rows_out, pairs, cin, cout)
    scratch_ref[9 * cin : total] = terms_ref[...]
    scratch_ref[total:] = jnp.zeros((scratch_ref.shape[0] - total, cout), jnp.float32)
    for index in range(count):
        chunks_ref[index] = scratch_ref[index * step : index * step + rows].astype(jnp.bfloat16)


def copies_kernel(chunks_ref, copies_ref):
    piece = jnp.sum(chunks_ref[...].astype(jnp.float32), axis=0).astype(jnp.bfloat16)
    for index in range(copies_ref.shape[0]):
        copies_ref[index] = piece


def finish_kernel(
    rim_ref, local_ref, grads_ref, later_ref, weight_ref, output_ref, grad_ref
):
    rows_out, pairs, cout = later_ref.shape
    cells = rows_out * pairs
    grads = with_next_pair(grads_ref[...].reshape(cells, cout), pairs)
    later = with_next_pair(later_ref[...].reshape(cells, cout), pairs)
    total = (
        forward_terms(rim_ref[0], weight_ref, 0, rows_out, pairs)
        + forward_terms(local_ref[0], weight_ref, 1, rows_out, pairs)
        + forward_terms(local_ref[1], weight_ref, 2, rows_out, pairs)
    )
    result = total[:, :cout] + from_previous_pair(total[:, cout:], pairs)
    output_ref[...] = result.astype(jnp.bfloat16).reshape(output_ref.shape)
    spilled = backward_terms(later, weight_ref, 0, pairs)
    own = backward_terms(grads, weight_ref, 2, pairs)
    planes = (
        backward_terms(grads, weight_ref, 1, pairs),
        (spilled[0] + own[0], spilled[1] + own[1]),
    )
    for plane, sides in enumerate(planes):
        for side, values in enumerate(sides):
            rounded = values.astype(jnp.bfloat16)
            for b in range(rows_out):
                grad_ref[plane, 2 * b + side] = rounded[b * pairs : (b + 1) * pairs]


def spread_kernel(step, factor, chunks_ref, grad_ref):
    for index in range(chunks_ref.shape[0]):
        block = chunks_ref[index].astype(jnp.float32)[:step]
        grad_ref[index * step : (index + 1) * step] = block * factor


def shards(volume, weight, cotangent):
    local = volume[0]
    grads = cotangent[0, 0]
    rows_out, pairs, cout = grads.shape
    cin = weight.shape[3]
    total = 27 * cin
    cells = rows_out * pairs
    count = math.prod(lax.axis_size(axis) for axis in SLAB)
    step = total // count
    rows = -(-step // 16) * 16
    devices = math.prod(lax.axis_size(axis) for axis in DP + SPACE)
    factor = 1.0 / math.sqrt(devices * cells)

    later = passed_along(grads, SPACE, -1)
    terms, plane = pl.pallas_call(
        own_kernel,
        out_shape=(
            jax.ShapeDtypeStruct((18 * cin, cout), jnp.float32),
            jax.ShapeDtypeStruct((1, *local.shape[1:]), jnp.bfloat16),
        ),
        cost_estimate=pl.CostEstimate(flops=300_000_000, bytes_accessed=2_000_000, transcendentals=0),
        compiler_params=pltpu.CompilerParams(vmem_limit_bytes=VMEM_BYTES),
        name="own",
    )(local, grads)
    chunks = pl.pallas_call(
        joined_kernel,
        out_shape=jax.ShapeDtypeStruct((count, rows, cout), jnp.bfloat16),
        scratch_shapes=[pltpu.VMEM((total + 16, cout), jnp.float32)],
        cost_estimate=pl.CostEstimate(flops=60_000_000, bytes_accessed=1_000_000, transcendentals=0),
        compiler_params=pltpu.CompilerParams(vmem_limit_bytes=VMEM_BYTES),
        name="joined",
    )(local, later, terms)
    lines = math.prod(lax.axis_size(axis) for axis in LINE)
    copies = pl.pallas_call(
        copies_kernel,
        out_shape=jax.ShapeDtypeStruct((lines, rows, cout), jnp.bfloat16),
        cost_estimate=pl.CostEstimate(flops=500_000, bytes_accessed=700_000, transcendentals=0),
        compiler_params=pltpu.CompilerParams(vmem_limit_bytes=VMEM_BYTES),
        name="copies",
    )(exchange(chunks, SLAB))
    copies, plane, later, local, grads = lax.optimization_barrier(
        (copies, plane, later, local, grads)
    )
    rim = passed_along(plane, SPACE, 1)
    piece = jnp.sum(exchange(copies, LINE).astype(jnp.float32), axis=0)

    output, grad_volume = pl.pallas_call(
        finish_kernel,
        out_shape=(
            jax.ShapeDtypeStruct((rows_out, pairs, cout), jnp.bfloat16),
            jax.ShapeDtypeStruct((2, 2 * rows_out, pairs, 2 * cin), jnp.bfloat16),
        ),
        cost_estimate=pl.CostEstimate(flops=400_000_000, bytes_accessed=1_500_000, transcendentals=0),
        compiler_params=pltpu.CompilerParams(vmem_limit_bytes=VMEM_BYTES),
        name="finish",
    )(rim, local, grads, later, weight)
    piece, output, grad_volume = lax.optimization_barrier((piece, output, grad_volume))
    copies = jnp.broadcast_to(piece.astype(jnp.bfloat16)[None], (count, rows, cout))
    gathered = exchange(copies, SLAB)
    parts = 4
    grad_weight = pl.pallas_call(
        functools.partial(spread_kernel, step, factor),
        grid=(parts,),
        in_specs=[pl.BlockSpec((count // parts, rows, cout), lambda part: (part, 0, 0))],
        out_specs=pl.BlockSpec((total // parts, cout), lambda part: (part, 0)),
        out_shape=jax.ShapeDtypeStruct((total, cout), jnp.float32),
        compiler_params=pltpu.CompilerParams(vmem_limit_bytes=VMEM_BYTES),
        name="spread_out",
    )(gathered)
    return (output[None, None], grad_volume[None], grad_weight.reshape(weight.shape))


def solution(mesh):
    fine = jax.sharding.Mesh(mesh.devices.reshape(SIZES), DP + SPACE)
    split = P(DP, SPACE, None, None, None)
    return jax.shard_map(
        shards,
        mesh=fine,
        in_specs=(split, P(), split),
        out_specs=(split, split, P()),
        check_vma=False,
    )
```
